32 devices in a mesh: grp: 4 (over y, core), dev: 8 (over z, x).
Axes of the slice: x: 2, y: 2, z: 4, core: 2. Of those that a mesh axis runs over, the one named last changes fastest.
Arguments:
- embeddings: bfloat16 [24576, 1024], P(('grp', 'dev')), may hold values from -6 to 6
- level_one: int32 [24576, 1], P(('grp', 'dev')), may hold values from 0 to 3; in each aligned block of 768 rows (0 to 767, 768 to 1535, ...) at most 384 rows name the same one
- centroids: bfloat16 [8192, 1024], P(('grp', 'dev')), may hold values from -6 to 6
Outputs:
- new_centroids: float32 [8192, 1024], P(('grp', 'dev'))
- column_mass: float32 [8192], P(('grp', 'dev'))
The draws below stay inside these ranges and needn't reach their ends.
Inputs may be any that keep to these rules, and one draw needn't show every extreme that they name: `level_one`: among the rows of one device no level-1 id appears more than 384 times, and every id appears somewhere.
All inputs are finite; a program needn't handle non-finite values.
Results may differ from the reference program's by a relative error of at most 0.018.
Values may be sent and summed in bfloat16 or wider, within the bound.
No kernel may reach another device: no remote copies, remote signals or barrier semaphores. Data moves between devices by JAX's collectives and lax.ppermute only.
A program may use at most 64 MiB of HBM per device.

```python
import math
import jax
import jax.numpy as jnp
import numpy as np
from jax import lax

D = 1024
K = 2048
R_DEV = 768
SWEEPS = 3
CAP = 384
ROWS = 24576
N_GRP = 4
N_DEV = 8


def level_of(rng, shape, shards, smallest, largest):
    loudness = 1.0
    for dim, shards_of in shards:
        draws = jax.random.uniform(jax.random.fold_in(jax.random.fold_in(rng, 6), dim), (shards_of,), jnp.float32, smallest / len(shards), largest / len(shards))
        loudness = loudness * jnp.repeat(jnp.exp(draws), shape[dim] // shards_of).reshape((-1,) + (1,) * (len(shape) - 1 - dim))
    return loudness


def deal_out(rng, own, number, rows, number_of, top, reach, lean):
    sequence = jax.random.permutation(rng, number_of)
    crowded, common = load_shares(number_of, rows * top, reach, lean, True), load_shares(number_of, rows * top, reach, lean, False)
    places = jnp.arange(number_of)

    def named(lengths, rotation):
        used = int((lengths > 0).sum())
        fixed = max(1, used // 4)
        passed = fixed + (places - fixed + rotation * (used - fixed)) % max(1, number_of - fixed)
        return jnp.zeros((number_of,), jnp.int32).at[sequence[jnp.where(places < fixed, places, passed)]].set(jnp.asarray(lengths, jnp.int32))

    lengths = jnp.where(number % 4 == 0, named(crowded, number // 4), named(common, number - number // 4 - 1))
    mixed = jax.random.permutation(jax.random.fold_in(own, 3), number_of)
    giver, receiver = mixed[0:number_of // 2 * 2:2], mixed[1:number_of // 2 * 2:2]
    margin = jnp.minimum(lengths[giver] - 1, reach - lengths[receiver]) // 2
    margin = jnp.where((giver == sequence[0]) | (receiver == sequence[0]) | (lengths[receiver] == 0), 0, jnp.maximum(margin, 0))
    passed = jax.random.randint(jax.random.fold_in(own, 4), (number_of // 2,), 0, 1 << 20) % (margin + 1)
    lengths = lengths.at[giver].add(-passed).at[receiver].add(passed)
    labels = jnp.searchsorted(jnp.cumsum(lengths), jnp.arange(rows * top), side="right").astype(jnp.int32)
    listing = labels.reshape(top, rows).T
    listing = listing[jax.random.permutation(jax.random.fold_in(own, 1), rows)]
    rotation = jax.random.randint(jax.random.fold_in(own, 2), (rows, 1), 0, top)
    return jnp.take_along_axis(listing, (jnp.arange(top)[None, :] + rotation) % top, axis=1)


def load_shares(amount, total, reach, slope, full):
    loads = [(1 << 20) // math.isqrt(rank ** slope) + 1 for rank in range(1, amount + 1)]
    largest = reach if full else min(reach, max(-(-total // amount), total * loads[0] // sum(loads)))
    least = 1 if total - largest >= amount - 1 else 0
    counts, rest = [largest] + [least] * (amount - 1), total - largest - least * (amount - 1)
    while rest > 0:
        free = [i for i in range(1, amount) if counts[i] < largest] or [i for i in range(1, amount) if counts[i] < reach]
        whole, remaining = sum([loads[i] for i in free]), rest
        for i in free:
            extra = min(reach - counts[i], max(1, remaining * loads[i] // whole), rest)
            counts[i] = counts[i] + extra
            rest = rest - extra
    return np.array(counts)


def noise(rng, dims, spread, reach, cuts=(), dtype=jnp.bfloat16):
    gain = level_of(rng, dims, cuts, -0.22, 0.18) if cuts else 1.0
    values = jax.random.normal(rng, dims, jnp.float32) * spread * gain
    return jnp.minimum(jnp.maximum(values, -reach), reach).astype(dtype)


def setup_inputs(seed: int = 0) -> dict:
    seeds = jax.random.split(jax.random.key(seed), 4)
    embeddings = noise(seeds[0], (ROWS, D), 1.0, 6.0, ((0, 32),))
    level_one_keys = jax.random.split(jax.random.fold_in(seeds[1], 1), ROWS // R_DEV)
    level_one_turns = jax.random.permutation(jax.random.fold_in(seeds[1], 3), ROWS // R_DEV)
    level_one = jax.vmap(lambda own, number: deal_out(jax.random.fold_in(seeds[1], 2), own, number, R_DEV, N_GRP, 1, CAP, 2))(level_one_keys, level_one_turns).reshape((ROWS, 1))
    centroids = noise(seeds[2], (N_GRP * K, D), 1.0, 6.0, ((0, 32),))
    return {"embeddings": embeddings, "level_one": level_one, "centroids": centroids}


def rms_normalize(vectors):
    wide = vectors.astype(jnp.float32)
    inverse = lax.rsqrt(lax.optimization_barrier(jnp.mean(wide * wide, axis=-1, keepdims=True)) + 1e-06)
    return (wide * inverse).astype(jnp.bfloat16)

def balance(group_rows, valid_mask, cent_rows):
    normed = rms_normalize(group_rows)
    cent_normed = rms_normalize(cent_rows)
    scores = lax.dot_general(normed, cent_normed, (((1,), (1,)), ((), ())), preferred_element_type=jnp.float32)
    weights = (jnp.exp(scores * (3.0 / math.sqrt(D))) * valid_mask[:, None]).astype(jnp.bfloat16)
    wide = weights.astype(jnp.float32)
    row_scale = valid_mask
    column_scale = jnp.ones((K,), jnp.float32)
    for sweep_index in range(SWEEPS):
        column_total = lax.optimization_barrier(jnp.sum(wide * row_scale[:, None], axis=0))
        column_scale = 1.0 / column_total
        row_total = lax.optimization_barrier(jnp.sum(wide * column_scale[None, :], axis=1))
        row_scale = valid_mask / (row_total + 1.0 - valid_mask)
    transport = wide * row_scale[:, None] * column_scale[None, :]
    column_mass = lax.optimization_barrier(jnp.sum(transport, axis=0))
    shared = transport.astype(jnp.bfloat16)
    numerator = lax.dot_general(shared, group_rows, (((0,), (0,)), ((), ())), preferred_element_type=jnp.float32)
    return (numerator / column_mass[:, None], column_mass)

def reference(embeddings, level_one, centroids):
    level_ids = level_one[:, 0]
    slot_total = N_GRP * N_DEV * CAP
    centroid_list = []
    mass_list = []
    for group_index in range(N_GRP):
        inside = level_ids == group_index
        position = jnp.cumsum(inside.astype(jnp.int32)) - 1
        slot_index = jnp.where(inside, position, slot_total).astype(jnp.int32)
        group_rows = jnp.zeros((slot_total, D), jnp.bfloat16).at[slot_index].set(embeddings, mode='drop')
        valid_mask = jnp.zeros((slot_total,), jnp.float32).at[slot_index].set(1.0, mode='drop')
        cent_rows = centroids[group_index * K:(group_index + 1) * K]
        updated, column_mass = balance(group_rows, valid_mask, cent_rows)
        centroid_list.append(updated)
        mass_list.append(column_mass)
    return (jnp.concatenate(centroid_list, axis=0), jnp.concatenate(mass_list, axis=0))
```

```python
import functools
import math

import jax
import jax.numpy as jnp
from jax import lax
from jax.experimental import pallas as pl
from jax.experimental.pallas import tpu as pltpu
from jax.sharding import PartitionSpec as P

SWEEPS = 3
EMPTY = 64.0
AXES = ("grp", "dev")
F32 = jnp.float32
BF16 = jnp.bfloat16
NT = (((1,), (1,)), ((), ()))
NN = (((1,), (0,)), ((), ()))
VMEM = pl.BlockSpec(memory_space=pltpu.VMEM)
PARAMS = pltpu.CompilerParams(vmem_limit_bytes=40 * 1024 * 1024)


def permutation(groups, peers, move):
    pairs = []
    for grp in range(groups):
        for dev in range(peers):
            pair, side, place, half = move(grp // 2, grp % 2, dev // 2, dev % 2)
            pairs.append((grp * peers + dev, (2 * pair + side) * peers + 2 * place + half))
    return pairs


class Routes:
    def __init__(self, groups, peers):
        self.ring = peers // 2
        make = functools.partial(permutation, groups, peers)
        turn = self.ring
        self.swap = make(lambda p, s, z, h: (p, h, z, s))
        self.core = make(lambda p, s, z, h: (p, 1 - s, z, h))
        self.shift = [make(lambda p, s, z, h, t=t: (p, s, (z + t) % turn, h)) for t in range(turn)]
        self.home = make(lambda p, s, z, h: (p, h, (z + 1) % turn, s))
        self.cluster = [
            make(lambda p, s, z, h, d=d: ((2 * p + h ^ d) // 2, s, z, (2 * p + h ^ d) % 2))
            for d in range(groups)
        ]


def send(value, route):
    return lax.ppermute(value, AXES, route)


def unit(rows):
    wide = rows.astype(F32)
    inverse = lax.rsqrt(jnp.mean(wide * wide, axis=-1, keepdims=True) + 1e-06)
    return (wide * inverse).astype(BF16)


def unit_kernel(rows_ref, out_ref):
    out_ref[...] = unit(rows_ref[...])


def pack_kernel(mine_ref, level_ref, rows_ref, *outs):
    groups = len(outs)
    count, capacity = rows_ref.shape[0], outs[0].shape[0]
    relative = level_ref[...] ^ mine_ref[0]
    member = (lax.broadcasted_iota(jnp.int32, (8, count), 0) == relative).astype(F32)
    upto = lax.broadcasted_iota(jnp.int32, (count, count), 0) <= lax.broadcasted_iota(
        jnp.int32, (count, count), 1
    )
    running = lax.dot_general(
        member.astype(BF16), upto.astype(F32).astype(BF16), NN, preferred_element_type=F32
    )
    within = jnp.sum(member * running, axis=0, keepdims=True).astype(jnp.int32) - 1
    slots = lax.broadcasted_iota(jnp.int32, (capacity, count), 0)
    for d in range(groups):
        place = jnp.where(relative == d, within, -1)
        pick = (slots == place).astype(F32)
        filled = jnp.sum(pick, axis=1, keepdims=True)
        picked = lax.dot_general(pick.astype(BF16), rows_ref[...], NN, preferred_element_type=F32)
        outs[d][...] = (picked + (1.0 - filled) * EMPTY).astype(BF16)


def prepare_kernel(*refs, first):
    one_ref, two_ref = refs[0], refs[1]
    unit_ref, valid_ref, turned_ref = refs[-3:]
    height = one_ref.shape[0]
    for j, ref in enumerate((one_ref, two_ref)):
        rows = ref[...]
        span = pl.ds(j * height, height)
        unit_ref[span, :] = unit(rows)
        present = (rows[:, 0:1].astype(F32) < 0.5 * EMPTY).astype(F32)
        valid_ref[span, :] = jnp.broadcast_to(present, (height, 128))
    both = jnp.concatenate([one_ref[...], two_ref[...]], axis=0)
    turned_ref[...] = both.T


def scores_kernel(rows_ref, valid_ref, mine_ref, other_ref, weights_ref, total_ref):
    width = mine_ref.shape[0]
    factor = 3.0 / math.sqrt(rows_ref.shape[1])

    @pl.when(pl.program_id(0) == 0)
    def _():
        total_ref[...] = jnp.zeros_like(total_ref)

    for j, ref in enumerate((mine_ref, other_ref)):
        span = pl.ds(j * width, width)
        scores = lax.dot_general(rows_ref[...], ref[...], NT, preferred_element_type=F32)
        weights = (jnp.exp(scores * factor) * valid_ref[:, 0:1]).astype(BF16)
        weights_ref[:, span] = weights
        total_ref[:, span] += jnp.sum(weights.astype(F32), axis=0, keepdims=True)


def join_kernel(part_ref, other_ref, out_ref, *, ring):
    width = part_ref.shape[1] // (2 * ring)
    for j in range(2 * ring):
        here, there = pl.ds(j * width, width), pl.ds((j ^ 1) * width, width)
        out_ref[:, here] = part_ref[:, here] + other_ref[:, there]


def inverse_totals(totals, scale_ref):
    ring = len(totals)
    width = scale_ref.shape[1] // ring
    for s in range(ring):
        total = totals[0][:, pl.ds(s * width, width)]
        for t in range(1, ring):
            total = total + totals[t][:, pl.ds((s - t) % ring * width, width)]
        scale_ref[:, pl.ds(s * width, width)] = 1.0 / total


STRIP = 32


def row_scales(chunks, scale_ref, start):
    width = chunks[0].shape[1]
    acc = jnp.zeros((STRIP, 128), F32)
    for s, ref in enumerate(chunks):
        wide = ref[pl.ds(start, STRIP), :].astype(F32) * scale_ref[:, pl.ds(s * width, width)]
        for j in range(width // 128):
            acc = acc + wide[:, j * 128 : (j + 1) * 128]
    total = jnp.sum(acc, axis=1, keepdims=True)
    return jnp.where(total > 0.0, 1.0 / total, 0.0)


def add_columns(chunks, row_scale, start, sums_ref):
    width = chunks[0].shape[1]
    for s, ref in enumerate(chunks):
        wide = ref[pl.ds(start, STRIP), :].astype(F32) * row_scale
        part = wide[0:8]
        for j in range(1, STRIP // 8):
            part = part + wide[8 * j : 8 * j + 8]
        sums_ref[:, pl.ds(s * width, width)] += part


def sweep_kernel(*refs, ring, last):
    totals, chunks = refs[:ring], refs[ring : 2 * ring]
    if last:
        out_ref, rows_ref, scale_ref, sums_ref = refs[2 * ring :]
    else:
        out_ref, scale_ref, sums_ref = refs[2 * ring :]

    @pl.when(pl.program_id(0) == 0)
    def _():
        sums_ref[...] = jnp.zeros_like(sums_ref)
        inverse_totals(totals, scale_ref)

    def strip(i, carry):
        start = pl.multiple_of(i * STRIP, STRIP)
        row_scale = row_scales(chunks, scale_ref, start)
        if last:
            rows_ref[pl.ds(start, STRIP), :] = jnp.broadcast_to(row_scale, (STRIP, 128))
        add_columns(chunks, row_scale, start, sums_ref)
        return carry

    lax.fori_loop(0, chunks[0].shape[0] // STRIP, strip, 0, unroll=2)

    @pl.when(pl.program_id(0) == pl.num_programs(0) - 1)
    def _():
        sums = jnp.sum(sums_ref[...], axis=0, keepdims=True)
        out_ref[...] = sums * scale_ref[...] if last else sums


def numerator_kernel(turned_ref, weights_ref, rows_ref, scale_ref, *refs):
    outs, shared_ref = refs[:-1], refs[-1]
    slots, width = weights_ref.shape
    block = slots // 6

    for i in range(6):
        span = pl.ds(i * block, block)
        wide = weights_ref[span, :].astype(F32)
        shared_ref[span, :] = (wide * rows_ref[span, 0:1] * scale_ref[...]).astype(BF16)
    height = outs[0].shape[0]
    step = 256
    for j in range(len(outs) // 2):
        for i in range(height // step):
            part = lax.dot_general(
                turned_ref[pl.ds(j * height + i * step, step), :],
                shared_ref[...],
                NN,
                preferred_element_type=F32,
            ).astype(BF16)
            outs[2 * j][pl.ds(i * step, step), :] = part[:, : width // 2]
            outs[2 * j + 1][pl.ds(i * step, step), :] = part[:, width // 2 :]


def finish_kernel(mass_ref, *refs):
    out_ref = refs[-1]
    height = refs[0].shape[0]
    inverse = 1.0 / mass_ref[...]
    half = len(refs) // 2
    for j in range(half):
        total = refs[j][...].astype(F32) + refs[half + j][...].astype(F32)
        out_ref[:, pl.ds(j * height, height)] = (total * inverse).T


def call(kernel, outs, *args, **kwargs):
    return pl.pallas_call(kernel, out_shape=outs, compiler_params=PARAMS, **kwargs)(*args)


def shape(*dims, dtype=BF16):
    return jax.ShapeDtypeStruct(dims, dtype)


def prepare(one, two, index, count, carried):
    height, depth = 2 * one.shape[0], one.shape[1]
    outs = (
        shape(count * height, depth),
        shape(count * height, 128, dtype=F32),
        shape(depth, count * height),
    )
    out_specs = (
        pl.BlockSpec((height, depth), lambda i: (index, 0)),
        pl.BlockSpec((height, 128), lambda i: (index, 0)),
        pl.BlockSpec((depth, height), lambda i: (0, index)),
    )
    whole = pl.BlockSpec((height // 2, depth), lambda i: (0, 0))
    held = pl.BlockSpec(memory_space=pl.ANY)
    return call(
        functools.partial(prepare_kernel, first=not carried),
        outs,
        one,
        two,
        *carried,
        grid=(1,),
        in_specs=[whole, whole] + [held] * len(carried),
        out_specs=out_specs,
        input_output_aliases={2 + j: j for j in range(len(carried))},
        name="prepare_rows",
    )


def scores(rows, valid, mine, other):
    slots, depth = rows.shape
    width = 2 * mine.shape[0]
    block = slots // 4
    centroid = pl.BlockSpec(mine.shape, lambda i: (0, 0))
    return call(
        scores_kernel,
        (shape(slots, width), shape(1, width, dtype=F32)),
        rows,
        valid,
        mine,
        other,
        grid=(4,),
        in_specs=[
            pl.BlockSpec((block, depth), lambda i: (i, 0)),
            pl.BlockSpec((block, 128), lambda i: (i, 0)),
            centroid,
            centroid,
        ],
        out_specs=(
            pl.BlockSpec((block, width), lambda i: (i, 0)),
            pl.BlockSpec((1, width), lambda i: (0, 0)),
        ),
        name="weights",
        cost_estimate=pl.CostEstimate(
            flops=2 * slots * width * depth, bytes_accessed=6_000_000, transcendentals=slots * width
        ),
    )


def sweep(totals, chunks, last):
    ring = len(chunks)
    slots, width = chunks[0].shape
    block = slots // 6
    row = pl.BlockSpec((1, ring * width), lambda i: (0, 0))
    outs, out_specs = (shape(1, ring * width, dtype=F32),), (row,)
    if last:
        outs += (shape(slots, 128, dtype=F32), shape(1, ring * width, dtype=F32))
        out_specs += (pl.BlockSpec((block, 128), lambda i: (i, 0)), row)
        scratch = [pltpu.VMEM((8, ring * width), F32)]
    else:
        scratch = [pltpu.VMEM((1, ring * width), F32), pltpu.VMEM((8, ring * width), F32)]
    return call(
        functools.partial(sweep_kernel, ring=ring, last=last),
        outs,
        *totals,
        *chunks,
        grid=(6,),
        in_specs=[row] * ring + [pl.BlockSpec((block, width), lambda i: (i, 0))] * ring,
        out_specs=out_specs,
        scratch_shapes=scratch,
        name="last_sweep" if last else "sweep",
    )


def numerator(turned, weights, rows, scale, index, parts):
    slots, width = weights.shape
    depth = turned.shape[0]
    whole = lambda a: pl.BlockSpec(a.shape, lambda i: (0, 0))
    out = shape(depth // parts, width // 2)
    return call(
        numerator_kernel,
        (out,) * (2 * parts),
        turned,
        weights,
        rows,
        scale,
        grid=(1,),
        in_specs=[
            whole(turned),
            whole(weights),
            whole(rows),
            pl.BlockSpec((1, width), lambda i: (0, index)),
        ],
        out_specs=(pl.BlockSpec(out.shape, lambda i: (0, 0)),) * (2 * parts),
        scratch_shapes=[pltpu.VMEM((slots, width), BF16)],
        name="numerator",
        cost_estimate=pl.CostEstimate(
            flops=2 * slots * width * depth, bytes_accessed=8_000_000, transcendentals=0
        ),
    )


def add(*terms):
    total = terms[0].astype(F32)
    for term in terms[1:]:
        total = total + term.astype(F32)
    return total.astype(BF16)


def body(embeddings, level_one, centroids):
    groups, peers = lax.axis_size("grp"), lax.axis_size("dev")
    routes = Routes(groups, peers)
    ring = routes.ring
    count, depth = embeddings.shape
    capacity = 2 * count // groups
    owned = centroids.shape[0]
    parts = 2
    piece = owned // parts

    own = call(unit_kernel, shape(owned, depth), centroids, name="unit_centroids")
    own = send(own, routes.swap)
    pieces = [[own[j * piece : (j + 1) * piece] for j in range(parts)]]
    for s in range(1, ring):
        pieces.append([send(p, routes.shift[1]) for p in pieces[-1]])
    mine = [own] + [jnp.concatenate(p, axis=0) for p in pieces[1:]]
    other = [send(m, routes.core) for m in mine]

    cluster = lax.axis_index("grp") // 2 * 2 + lax.axis_index("dev") % 2
    packed = call(
        pack_kernel,
        (shape(capacity, depth),) * groups,
        cluster.astype(jnp.int32).reshape(1),
        level_one.reshape(1, count),
        embeddings,
        in_specs=[pl.BlockSpec(memory_space=pltpu.SMEM), VMEM, VMEM],
        out_specs=(VMEM,) * groups,
        name="pack_rows",
    )
    arrived = [packed[0]] + [send(packed[d], routes.cluster[d]) for d in range(1, groups)]
    held = ()
    for j in range(groups // 2):
        held = prepare(arrived[2 * j], arrived[2 * j + 1], j, groups // 2, held)
    rows, valid, turned = held

    chunks, sums = [], []
    for s in range(ring):
        weights, total = scores(rows, valid, mine[s], other[s])
        chunks.append(weights)
        sums.append(total)
    part = jnp.concatenate(sums, axis=1)

    def everywhere(part):
        chip = call(
            functools.partial(join_kernel, ring=ring),
            shape(*part.shape, dtype=F32),
            part,
            send(part, routes.core),
            name="join_cores",
        )
        return [chip] + [send(chip, routes.shift[t]) for t in range(1, ring)]

    for _ in range(SWEEPS - 1):
        (part,) = sweep(everywhere(part), chunks, last=False)
    mass_part, row_scale, column_scale = sweep(everywhere(part), chunks, last=True)

    moving = None
    for s in [*range(1, ring), 0]:
        outs = numerator(turned, chunks[s], row_scale, column_scale, s, parts)
        terms = [(outs[2 * j], send(outs[2 * j + 1], routes.core)) for j in range(parts)]
        if s == 1:
            moving = [send(add(*t), routes.home if ring == 2 else routes.shift[1]) for t in terms]
        elif s > 1:
            route = routes.home if s == ring - 1 else routes.shift[1]
            moving = [send(add(m, *t), route) for m, t in zip(moving, terms)]
        else:
            kept = [send(add(*t), routes.swap) for t in terms]

    masses = everywhere(mass_part)
    mass = masses[0][:, :owned]
    for t in range(1, ring):
        start = (-t) % ring * 2 * owned
        mass = mass + masses[t][:, start : start + owned]
    mass = send(mass, routes.swap)
    updated = call(
        finish_kernel, shape(owned, depth, dtype=F32), mass, *moving, *kept, name="finish"
    )
    return updated, mass.reshape(owned)


def solution(mesh):
    in_specs = (P(AXES, None), P(AXES, None), P(AXES, None))
    out_specs = (P(AXES, None), P(AXES))
    return jax.shard_map(body, mesh=mesh, in_specs=in_specs, out_specs=out_specs, check_vma=False)
```

```python
import functools
import math

import jax
import jax.numpy as jnp
from jax import lax
from jax.experimental import pallas as pl
from jax.experimental.pallas import tpu as pltpu
from jax.sharding import PartitionSpec as P

SWEEPS = 3
EMPTY = 64.0
AXES = ("grp", "dev")
F32 = jnp.float32
BF16 = jnp.bfloat16
NT = (((1,), (1,)), ((), ()))
NN = (((1,), (0,)), ((), ()))
VMEM = pl.BlockSpec(memory_space=pltpu.VMEM)
SMEM = pl.BlockSpec(memory_space=pltpu.SMEM)
HELD = pl.BlockSpec(memory_space=pl.ANY)
PARAMS = pltpu.CompilerParams(vmem_limit_bytes=16 * 1024 * 1024)


def permutation(groups, peers, move):
    pairs = []
    for grp in range(groups):
        for dev in range(peers):
            target = move(grp // 2, grp % 2, dev // 2, dev % 2)
            if target is None:
                continue
            pair, side, place, half = target
            pairs.append((grp * peers + dev, (2 * pair + side) * peers + 2 * place + half))
    return pairs


class Routes:
    def __init__(self, groups, peers):
        self.ring = peers // 2
        make = functools.partial(permutation, groups, peers)
        turn = self.ring
        self.swap = make(lambda p, s, z, h: (p, h, z, s))
        self.core = make(lambda p, s, z, h: (p, 1 - s, z, h))
        self.shift = [make(lambda p, s, z, h, t=t: (p, s, (z + t) % turn, h)) for t in range(turn)]
        self.swap = make(lambda p, s, z, h: (p, h, z, s))
        self.both = [
            make(lambda p, s, z, h, t=t: (p, s, (z + (-t if s else t)) % turn, h))
            for t in range(turn // 2 + 1)
        ]
        self.home = make(lambda p, s, z, h: (p, h, (z + 1) % turn, s))
        self.cluster = [
            make(lambda p, s, z, h, d=d: ((2 * p + h ^ d) // 2, s, z, (2 * p + h ^ d) % 2))
            for d in range(groups)
        ]


def send(value, route):
    return lax.ppermute(value, AXES, route)


def call(kernel, outs, args, after=(), specs=None, alias=None, out_specs=None, **kwargs):
    args, after = list(args), list(after)

    def ordered(*refs):
        kernel(*refs[: len(args)], *refs[len(args) + len(after) :])

    return pl.pallas_call(
        ordered,
        out_shape=outs,
        in_specs=(specs or [VMEM] * len(args)) + [HELD] * len(after),
        out_specs=out_specs or jax.tree.map(lambda _: VMEM, outs),
        input_output_aliases=alias or {},
        compiler_params=PARAMS,
        **kwargs,
    )(*args, *after)


def cost(m, n, k):
    return pl.CostEstimate(
        flops=2 * m * n * k, bytes_accessed=2 * (m * n + n * k + m * k), transcendentals=0
    )


WAIT = pl.CostEstimate(flops=2 * 10**10, bytes_accessed=0, transcendentals=0)


def tie(values, after):
    values, after = list(values), list(after)
    return pl.pallas_call(
        lambda *refs: None,
        out_shape=tuple(jax.ShapeDtypeStruct(v.shape, v.dtype) for v in values),
        in_specs=[HELD] * (len(values) + len(after)),
        out_specs=(HELD,) * len(values),
        input_output_aliases={j: j for j in range(len(values))},
        compiler_params=PARAMS,
        cost_estimate=WAIT,
        name="tie",
    )(*values, *after)


def shape(*dims, dtype=BF16):
    return jax.ShapeDtypeStruct(dims, dtype)


def exact(line):
    high = line.astype(BF16).astype(F32)
    middle = (line - high).astype(BF16).astype(F32)
    low = line - high - middle
    at = lax.broadcasted_iota(jnp.int32, (16, line.shape[1]), 0)
    split = jnp.where(at == 0, high, jnp.where(at == 1, middle, jnp.where(at == 2, low, 0.0)))
    return split.astype(BF16)


def fast_here():
    return lax.axis_index("grp") % 2 == lax.axis_index("dev") % 2


def cluster_here():
    return lax.axis_index("grp") // 2 * 2 + lax.axis_index("dev") % 2


def unit(rows):
    wide = rows.astype(F32)
    inverse = lax.rsqrt(jnp.mean(wide * wide, axis=-1, keepdims=True) + 1e-06)
    return (wide * inverse).astype(BF16)


def unit_kernel(rows_ref, *outs):
    height = outs[0].shape[0]
    for j, out_ref in enumerate(outs):
        out_ref[...] = unit(rows_ref[pl.ds(j * height, height), :])


def rank_kernel(level_ref, place_ref):
    lines, count = place_ref.shape
    relative = level_ref[...] ^ cluster_here()
    member = lax.broadcasted_iota(jnp.int32, (lines, count), 0) == relative
    upto = lax.broadcasted_iota(jnp.int32, (count, count), 0) <= lax.broadcasted_iota(
        jnp.int32, (count, count), 1
    )
    running = lax.dot_general(
        member.astype(F32).astype(BF16),
        upto.astype(F32).astype(BF16),
        NN,
        preferred_element_type=F32,
    )
    place_ref[...] = jnp.where(member, running.astype(jnp.int32) - 1, -1)


def pick_kernel(place_ref, rows_ref, out_ref, *, which):
    capacity, count = out_ref.shape[0], rows_ref.shape[0]
    slots = lax.broadcasted_iota(jnp.int32, (capacity, count), 0)
    pick = (slots == place_ref[which : which + 1, :]).astype(F32)
    filled = jnp.sum(pick, axis=1, keepdims=True)
    picked = lax.dot_general(pick.astype(BF16), rows_ref[...], NN, preferred_element_type=F32)
    out_ref[...] = (picked + (1.0 - filled) * EMPTY).astype(BF16)


def weights_kernel(*refs, raw, lines, columns, carried, groups):
    *refs, unit_ref, valid_ref, weights_ref, sums_ref = refs
    inputs = refs[4 if carried else 0 :]
    pieces = inputs[len(raw) :]
    each = len(pieces) // (2 * len(columns))
    height = pieces[0].shape[0]
    capacity, depth = unit_ref.shape[0] // groups, unit_ref.shape[1]
    pick = lax.broadcasted_iota(jnp.int32, (16, 128), 0) + lax.broadcasted_iota(
        jnp.int32, (16, 128), 1
    )
    pick = jnp.where(pick == 0, 1.0, 0.0).astype(BF16)
    for ref, d in zip(inputs, raw):
        span = pl.ds(d * capacity, capacity)
        rows = ref[...]
        present = (rows[:, 0:1].astype(F32) < 0.5 * EMPTY).astype(F32)
        unit_ref[span, :] = unit(rows.astype(F32) * present)
        across = jnp.broadcast_to(present, (capacity, 128)).astype(BF16)
        valid = lax.dot_general(pick, across, NT, preferred_element_type=F32)
        valid_ref[:, span] = valid[0:1]

    fast = fast_here()
    half = each * height
    group = max(1, 512 // (2 * half))
    factor = 3.0 / math.sqrt(depth) * math.log2(math.e)
    for j in range(0, len(columns), group):
        block = []
        for k in range(j, min(j + group, len(columns))):
            refs = pieces[2 * each * k : 2 * each * (k + 1)]
            mine, other = (
                jnp.concatenate([ref[...] for ref in part], axis=0)
                for part in (refs[:each], refs[each:])
            )
            block += [jnp.where(fast, mine, other), jnp.where(fast, other, mine)]
        block = jnp.concatenate(block, axis=0)
        at = pl.ds(columns[j] * 2 * half, block.shape[0])
        for d in lines:
            span = pl.ds(d * capacity, capacity)
            scores = lax.dot_general(unit_ref[span, :], block, NT, preferred_element_type=F32)
            weights_ref[span, at] = jnp.exp2(scores * factor).astype(BF16)
    at = pl.ds(columns[0] * 2 * half, len(columns) * 2 * half)
    span = pl.ds(lines[0] * capacity, len(lines) * capacity)
    valid = jnp.broadcast_to(valid_ref[:, span], (16, len(lines) * capacity)).astype(BF16)
    sums = lax.dot_general(valid, weights_ref[span, at], NN, preferred_element_type=F32)[0:1]
    sums_ref[:, at] = sums if 0 in lines else sums_ref[:, at] + sums


def turn_kernel(*refs):
    rows, out_ref = refs[:-1], refs[-1]
    width = 2 * rows[0].shape[0]
    for j in range(len(rows) // 2):
        both = jnp.concatenate([rows[2 * j][...], rows[2 * j + 1][...]], axis=0)
        out_ref[:, pl.ds(j * width, width)] = both.T


def join_kernel(part_ref, other_ref, out_ref):
    out_ref[...] = part_ref[...] + other_ref[...]


def inverse_totals(totals, scale_ref):
    ring, width = len(totals), totals[0].shape[1] // len(totals)
    zero = lax.axis_index("grp") % 2 == 0
    for s in range(ring):

        def chunk(ref, t):
            return ref[:, pl.ds((s - t) % ring * width, width)]

        total = chunk(totals[0], 0) + chunk(totals[1], ring // 2)
        for t in range(1, ring // 2):
            near, far = totals[2 * t], totals[2 * t + 1]
            ahead = jnp.where(zero, chunk(near, t), chunk(far, t))
            behind = jnp.where(zero, chunk(far, -t), chunk(near, -t))
            total = total + (ahead + behind)
        scale_ref[:, pl.ds(s * width, width)] = 1.0 / total


def sweep_kernel(*refs, ring, last):
    valid_ref, weights_ref, *refs = refs
    totals = refs[:ring]
    if last:
        out_ref, rows_ref, scale_ref = refs[ring:]
    else:
        out_ref, scale_ref = refs[ring:]
    inverse_totals(totals, scale_ref)
    weights, valid = weights_ref[...], valid_ref[...]
    total = lax.dot_general(exact(scale_ref[...]), weights, NT, preferred_element_type=F32)
    total = jnp.sum(total, axis=0, keepdims=True)
    row_scale = valid / (total + 1.0 - valid)
    sums = lax.dot_general(exact(row_scale), weights, NN, preferred_element_type=F32)
    sums = jnp.sum(sums, axis=0, keepdims=True)
    if last:
        rows_ref[...] = row_scale
        out_ref[...] = sums * scale_ref[...]
    else:
        out_ref[...] = sums


def high_low(total, height):
    line = lax.broadcasted_iota(jnp.int32, (height, total.shape[1]), 0)
    high = total.astype(BF16).astype(F32)
    return jnp.where(line == 0, high, jnp.where(line == 1, total - high, 0.0)).astype(BF16)


def numerator_kernel(turned_ref, weights_ref, *refs, chunk, first, height, fresh):
    fast = fast_here()
    if fresh:
        rows_ref, scale_ref, mass_ref, scaled_ref, *outs = refs
        scaled = turned_ref[pl.ds(first, height), :].astype(F32) * rows_ref[...]
        scaled_ref[...] = scaled.astype(BF16)
    else:
        scale_ref, mass_ref, *outs = refs
        scaled_ref = turned_ref
    width = outs[0].shape[1]
    step = min(256, height)
    at = pl.ds(chunk * 2 * width, 2 * width)
    for i in range(height // step):
        part = lax.dot_general(
            scaled_ref[pl.ds(i * step, step), :],
            weights_ref[:, at],
            NN,
            preferred_element_type=F32,
        )
        part = (part * scale_ref[:, at]).astype(BF16)
        one, two = part[:, :width], part[:, width:]
        outs[0][pl.ds(i * step, step), :] = jnp.where(fast, one, two)
        outs[1][pl.ds(i * step, step), :] = jnp.where(fast, two, one)
    extra = outs[0].shape[0] - height
    if extra:
        masses = [mass_ref[:, pl.ds((2 * chunk + k) * width, width)] for k in range(2)]
        one, two = (high_low(mass, extra) for mass in masses)
        outs[0][pl.ds(height, extra), :] = jnp.where(fast, one, two)
        outs[1][pl.ds(height, extra), :] = jnp.where(fast, two, one)


def total_of(refs, height):
    total = refs[0][0:height, :].astype(F32)
    for ref in refs[1:]:
        total = total + ref[0:height, :].astype(F32)
    return total


def mass_of(refs, height):
    mass = 0.0
    for ref in refs:
        lines = ref[height : height + 16, :].astype(F32)
        mass = mass + (lines[0:1] + lines[1:2])
    return mass


def combine_kernel(*refs, height):
    out_ref = refs[-1]
    extra = out_ref.shape[0] - height
    out_ref[0:height, :] = total_of(refs[:-1], height).astype(BF16)
    if extra:
        out_ref[height : height + extra, :] = high_low(mass_of(refs[:-1], height), extra)


def finish_kernel(*refs, height):
    out_ref, mass_ref = refs[-2:]
    terms = refs[:-2]
    parts = len(terms) // 2
    mass = mass_of(terms[2 * parts - 2 :], height)
    mass_ref[...] = mass
    inverse = 1.0 / mass
    for j in range(parts):
        total = total_of(terms[2 * j : 2 * j + 2], height)
        out_ref[:, pl.ds(j * height, height)] = (total * inverse).T


def body(embeddings, level_one, centroids):
    groups, peers = lax.axis_size("grp"), lax.axis_size("dev")
    routes = Routes(groups, peers)
    ring = routes.ring
    count, depth = embeddings.shape
    capacity = 2 * count // groups
    slots = groups * capacity
    owned = centroids.shape[0]
    clusters = owned * peers
    parts = 2

    own = call(
        unit_kernel,
        (shape(owned // parts, depth),) * parts,
        [send(centroids, routes.swap)],
        name="unit_centroids",
        cost_estimate=WAIT,
    )
    mine = [own]
    for s in range(1, ring):
        mine.append([send(p, routes.shift[1]) for p in mine[-1]])
    other = [[send(p, routes.core) for p in m] for m in mine]

    place = call(
        rank_kernel,
        shape(-(-groups // 8) * 8, count, dtype=jnp.int32),
        [level_one.reshape(1, count)],
        name="rank_rows",
    )

    def pick(d, after=()):
        return call(
            functools.partial(pick_kernel, which=d),
            shape(capacity, depth),
            [place, embeddings],
            after=after,
            name="pick_rows",
        )

    arrived, packed = {}, ()
    for d in [*range(2, groups), 1, 0]:
        packed = (pick(d, packed),)
        arrived[d] = send(packed[0], routes.cluster[d]) if d else packed[0]

    state_shapes = (
        shape(slots, depth),
        shape(1, slots, dtype=F32),
        shape(slots, clusters),
        shape(1, clusters, dtype=F32),
    )

    def absorb(state, raw, lines, columns):
        pieces = [p for s in columns for part in (mine, other) for p in part[s]]
        rows = [arrived[d] for d in raw]
        return call(
            functools.partial(
                weights_kernel,
                raw=raw,
                lines=lines,
                columns=columns,
                carried=bool(state),
                groups=groups,
            ),
            state_shapes,
            [*state, *rows, *pieces],
            alias={j: j for j in range(len(state))},
            name="weights",
        )

    early = list(range(ring - 1))
    state = absorb((), [0], [0], early)
    rest = list(range(1, groups))
    waited = rest
    arrived.update(zip(waited, tie([arrived[d] for d in waited], ())))
    state = absorb(state, rest, rest, early)
    rows, valid, weights, part = absorb(state, [], [0, *rest], [ring - 1])
    turned = call(
        turn_kernel, shape(depth, slots), [arrived[d] for d in range(groups)], name="turn_rows"
    )

    def sweep(part, last):
        chip = call(
            join_kernel,
            shape(1, clusters, dtype=F32),
            [part, send(part, routes.core)],
            name="join_cores",
        )
        near = [send(chip, routes.both[t]) for t in range(1, ring // 2)]
        totals = [chip, send(chip, routes.shift[ring // 2])]
        for value in near:
            totals += [value, send(value, routes.core)]
        outs = (shape(1, clusters, dtype=F32),)
        if last:
            outs += (shape(1, slots, dtype=F32), shape(1, clusters, dtype=F32))
        return call(
            functools.partial(sweep_kernel, ring=ring, last=last),
            outs,
            [valid, weights, *totals],
            scratch_shapes=() if last else (pltpu.VMEM((1, clusters), F32),),
            name="last_sweep" if last else "sweep",
        )

    for _ in range(SWEEPS - 1):
        (part,) = sweep(part, last=False)
    mass_part, row_scale, column_scale = sweep(part, last=True)

    height = depth // parts
    tall = [height] * (parts - 1) + [height + 16]

    def numerator(s, j, after):
        fresh = scaled[j] is None
        args = [turned, weights, row_scale] if fresh else [scaled[j], weights]
        args = [*args, column_scale, mass_part]
        outs = (shape(tall[j], owned),) * 2
        if fresh:
            outs = (shape(height, slots), *outs)
        outs = call(
            functools.partial(
                numerator_kernel, chunk=s, first=j * height, height=height, fresh=fresh
            ),
            outs,
            args,
            after=after,
            name="numerator",
            cost_estimate=cost(height, 2 * owned, slots),
        )
        if fresh:
            scaled[j] = outs[0]
        return outs[-2], outs[-1]

    def combine(j, *terms):
        return call(
            functools.partial(combine_kernel, height=height),
            shape(tall[j], owned),
            terms,
            name="combine",
        )

    scaled = [None] * parts
    after, moving, kept = (), [()] * parts, []
    for s in [*range(1, ring), 0]:
        route = routes.swap if s == 0 else routes.home if s == ring - 1 else routes.shift[1]
        pairs = []
        for j in range(parts):
            kept_part, sent_part = numerator(s, j, after)
            pairs.append((kept_part, send(sent_part, routes.core)))
        if s == 0:
            kept = [send(combine(j, *pairs[j]), route) for j in range(parts)]
            continue
        added = [combine(j, *moving[j], *pairs[j]) for j in range(parts)]
        if s == 1:
            after = tuple(added)
        moving = [(send(a, route),) for a in added]

    updated, mass = call(
        functools.partial(finish_kernel, height=height),
        (shape(owned, depth, dtype=F32), shape(1, owned, dtype=F32)),
        [t for j in range(parts) for t in (moving[j][0], kept[j])],
        name="finish",
    )
    return updated, mass.reshape(owned)


def solution(mesh):
    in_specs = (P(AXES, None), P(AXES, None), P(AXES, None))
    out_specs = (P(AXES, None), P(AXES))
    return jax.shard_map(body, mesh=mesh, in_specs=in_specs, out_specs=out_specs, check_vma=False)
```

```python
import functools
import math

import jax
import jax.numpy as jnp
from jax import lax
from jax.experimental import pallas as pl
from jax.experimental.pallas import tpu as pltpu
from jax.sharding import PartitionSpec as P

SWEEPS = 3
EMPTY = 64.0
AXES = ("grp", "dev")
F32 = jnp.float32
BF16 = jnp.bfloat16
NT = (((1,), (1,)), ((), ()))
NN = (((1,), (0,)), ((), ()))
VMEM = pl.BlockSpec(memory_space=pltpu.VMEM)
SMEM = pl.BlockSpec(memory_space=pltpu.SMEM)
HELD = pl.BlockSpec(memory_space=pl.ANY)
PARAMS = pltpu.CompilerParams(vmem_limit_bytes=16 * 1024 * 1024)


def permutation(groups, peers, move):
    pairs = []
    for grp in range(groups):
        for dev in range(peers):
            target = move(grp // 2, grp % 2, dev // 2, dev % 2)
            if target is None:
                continue
            pair, side, place, half = target
            pairs.append((grp * peers + dev, (2 * pair + side) * peers + 2 * place + half))
    return pairs


class Routes:
    def __init__(self, groups, peers):
        self.ring = peers // 2
        make = functools.partial(permutation, groups, peers)
        turn = self.ring
        self.swap = make(lambda p, s, z, h: (p, h, z, s))
        self.core = make(lambda p, s, z, h: (p, 1 - s, z, h))
        self.shift = [make(lambda p, s, z, h, t=t: (p, s, (z + t) % turn, h)) for t in range(turn)]
        self.swap = make(lambda p, s, z, h: (p, h, z, s))
        self.both = [
            make(lambda p, s, z, h, t=t: (p, s, (z + (-t if s else t)) % turn, h))
            for t in range(turn // 2 + 1)
        ]
        self.home = make(lambda p, s, z, h: (p, h, (z + 1) % turn, s))
        self.cluster = [
            make(lambda p, s, z, h, d=d: ((2 * p + h ^ d) // 2, s, z, (2 * p + h ^ d) % 2))
            for d in range(groups)
        ]


def send(value, route):
    return lax.ppermute(value, AXES, route)


BRIEF = pl.CostEstimate(flops=1, bytes_accessed=1, transcendentals=0)
TURN = pl.CostEstimate(flops=6 * 10**9, bytes_accessed=1, transcendentals=0)
WAIT = pl.CostEstimate(flops=2 * 10**10, bytes_accessed=0, transcendentals=0)


def call(kernel, outs, args, after=(), specs=None, alias=None, out_specs=None, **kwargs):
    args, after = list(args), list(after)

    def ordered(*refs):
        kernel(*refs[: len(args)], *refs[len(args) + len(after) :])

    return pl.pallas_call(
        ordered,
        out_shape=outs,
        in_specs=(specs or [VMEM] * len(args)) + [HELD] * len(after),
        out_specs=out_specs or jax.tree.map(lambda _: VMEM, outs),
        input_output_aliases=alias or {},
        compiler_params=PARAMS,
        **kwargs,
    )(*args, *after)


def cost(m, n, k):
    return pl.CostEstimate(
        flops=2 * m * n * k, bytes_accessed=2 * (m * n + n * k + m * k), transcendentals=0
    )


def tie(values, after, hint=WAIT):
    values, after = list(values), list(after)
    return pl.pallas_call(
        lambda *refs: None,
        out_shape=tuple(jax.ShapeDtypeStruct(v.shape, v.dtype) for v in values),
        in_specs=[HELD] * (len(values) + len(after)),
        out_specs=(HELD,) * len(values),
        input_output_aliases={j: j for j in range(len(values))},
        compiler_params=PARAMS,
        cost_estimate=hint,
        name="tie",
    )(*values, *after)


def shape(*dims, dtype=BF16):
    return jax.ShapeDtypeStruct(dims, dtype)


def exact(line):
    high = line.astype(BF16).astype(F32)
    middle = (line - high).astype(BF16).astype(F32)
    low = line - high - middle
    at = lax.broadcasted_iota(jnp.int32, (16, line.shape[1]), 0)
    split = jnp.where(at == 0, high, jnp.where(at == 1, middle, jnp.where(at == 2, low, 0.0)))
    return split.astype(BF16)


def fast_here():
    return lax.axis_index("grp") % 2 == lax.axis_index("dev") % 2


def cluster_here():
    return lax.axis_index("grp") // 2 * 2 + lax.axis_index("dev") % 2


def unit(rows):
    wide = rows.astype(F32)
    inverse = lax.rsqrt(jnp.mean(wide * wide, axis=-1, keepdims=True) + 1e-06)
    return (wide * inverse).astype(BF16)


def unit_kernel(rows_ref, *outs):
    height = outs[0].shape[0]
    for j, out_ref in enumerate(outs):
        out_ref[...] = unit(rows_ref[pl.ds(j * height, height), :])


def rank_kernel(level_ref, place_ref):
    lines, count = place_ref.shape
    relative = level_ref[...] ^ cluster_here()
    member = lax.broadcasted_iota(jnp.int32, (lines, count), 0) == relative
    upto = lax.broadcasted_iota(jnp.int32, (count, count), 0) <= lax.broadcasted_iota(
        jnp.int32, (count, count), 1
    )
    running = lax.dot_general(
        member.astype(F32).astype(BF16),
        upto.astype(F32).astype(BF16),
        NN,
        preferred_element_type=F32,
    )
    place_ref[...] = jnp.where(member, running.astype(jnp.int32) - 1, -1)


def pick_kernel(place_ref, rows_ref, out_ref, *, which):
    capacity, count = out_ref.shape[0], rows_ref.shape[0]
    slots = lax.broadcasted_iota(jnp.int32, (capacity, count), 0)
    pick = (slots == place_ref[which : which + 1, :]).astype(F32)
    filled = jnp.sum(pick, axis=1, keepdims=True)
    picked = lax.dot_general(pick.astype(BF16), rows_ref[...], NN, preferred_element_type=F32)
    out_ref[...] = (picked + (1.0 - filled) * EMPTY).astype(BF16)


def weights_kernel(*refs, raw, lines, columns, carried, groups):
    *refs, unit_ref, valid_ref, weights_ref, sums_ref = refs
    inputs = refs[4 if carried else 0 :]
    pieces = inputs[len(raw) :]
    each = len(pieces) // (2 * len(columns))
    height = pieces[0].shape[0]
    capacity, depth = unit_ref.shape[0] // groups, unit_ref.shape[1]
    pick = lax.broadcasted_iota(jnp.int32, (16, 128), 0) + lax.broadcasted_iota(
        jnp.int32, (16, 128), 1
    )
    pick = jnp.where(pick == 0, 1.0, 0.0).astype(BF16)
    for ref, d in zip(inputs, raw):
        span = pl.ds(d * capacity, capacity)
        rows = ref[...]
        present = (rows[:, 0:1].astype(F32) < 0.5 * EMPTY).astype(F32)
        unit_ref[span, :] = unit(rows.astype(F32) * present)
        across = jnp.broadcast_to(present, (capacity, 128)).astype(BF16)
        valid = lax.dot_general(pick, across, NT, preferred_element_type=F32)
        valid_ref[:, span] = valid[0:1]

    fast = fast_here()
    half = each * height
    group = max(1, 512 // (2 * half))
    factor = 3.0 / math.sqrt(depth) * math.log2(math.e)
    for j in range(0, len(columns), group):
        block = []
        for k in range(j, min(j + group, len(columns))):
            refs = pieces[2 * each * k : 2 * each * (k + 1)]
            mine, other = (
                jnp.concatenate([ref[...] for ref in part], axis=0)
                for part in (refs[:each], refs[each:])
            )
            block += [jnp.where(fast, mine, other), jnp.where(fast, other, mine)]
        block = jnp.concatenate(block, axis=0)
        at = pl.ds(columns[j] * 2 * half, block.shape[0])
        for d in lines:
            span = pl.ds(d * capacity, capacity)
            scores = lax.dot_general(unit_ref[span, :], block, NT, preferred_element_type=F32)
            weights_ref[span, at] = jnp.exp2(scores * factor).astype(BF16)
    at = pl.ds(columns[0] * 2 * half, len(columns) * 2 * half)
    span = pl.ds(lines[0] * capacity, len(lines) * capacity)
    valid = jnp.broadcast_to(valid_ref[:, span], (16, len(lines) * capacity)).astype(BF16)
    sums = lax.dot_general(valid, weights_ref[span, at], NN, preferred_element_type=F32)[0:1]
    sums_ref[:, at] = sums if 0 in lines else sums_ref[:, at] + sums


def turn_kernel(*refs):
    rows, out_ref = refs[:-1], refs[-1]
    width = 2 * rows[0].shape[0]
    for j in range(len(rows) // 2):
        both = jnp.concatenate([rows[2 * j][...], rows[2 * j + 1][...]], axis=0)
        out_ref[:, pl.ds(j * width, width)] = both.T


def join_kernel(part_ref, other_ref, out_ref):
    out_ref[...] = part_ref[...] + other_ref[...]


def inverse_totals(totals, scale_ref):
    ring, width = len(totals), totals[0].shape[1] // len(totals)
    zero = lax.axis_index("grp") % 2 == 0
    for s in range(ring):

        def chunk(ref, t):
            return ref[:, pl.ds((s - t) % ring * width, width)]

        total = chunk(totals[0], 0) + chunk(totals[1], ring // 2)
        for t in range(1, ring // 2):
            near, far = totals[2 * t], totals[2 * t + 1]
            ahead = jnp.where(zero, chunk(near, t), chunk(far, t))
            behind = jnp.where(zero, chunk(far, -t), chunk(near, -t))
            total = total + (ahead + behind)
        scale_ref[:, pl.ds(s * width, width)] = 1.0 / total


def sweep_kernel(*refs, ring, last):
    valid_ref, weights_ref, *refs = refs
    totals = refs[:ring]
    if last:
        out_ref, rows_ref, scale_ref = refs[ring:]
    else:
        out_ref, scale_ref = refs[ring:]
    inverse_totals(totals, scale_ref)
    weights, valid = weights_ref[...], valid_ref[...]
    total = lax.dot_general(exact(scale_ref[...]), weights, NT, preferred_element_type=F32)
    total = jnp.sum(total, axis=0, keepdims=True)
    row_scale = valid / (total + 1.0 - valid)
    sums = lax.dot_general(exact(row_scale), weights, NN, preferred_element_type=F32)
    sums = jnp.sum(sums, axis=0, keepdims=True)
    if last:
        rows_ref[...] = row_scale
        out_ref[...] = sums * scale_ref[...]
    else:
        out_ref[...] = sums


def high_low(total, height):
    line = lax.broadcasted_iota(jnp.int32, (height, total.shape[1]), 0)
    high = total.astype(BF16).astype(F32)
    return jnp.where(line == 0, high, jnp.where(line == 1, total - high, 0.0)).astype(BF16)


def numerator_kernel(turned_ref, weights_ref, *refs, chunk, first, height, fresh):
    fast = fast_here()
    if fresh:
        rows_ref, scale_ref, mass_ref, scaled_ref, *outs = refs
        scaled = turned_ref[pl.ds(first, height), :].astype(F32) * rows_ref[...]
        scaled_ref[...] = scaled.astype(BF16)
    else:
        scale_ref, mass_ref, *outs = refs
        scaled_ref = turned_ref
    width = outs[0].shape[1]
    step = height if height <= 384 else height // 2
    at = pl.ds(chunk * 2 * width, 2 * width)
    for i in range(height // step):
        part = lax.dot_general(
            scaled_ref[pl.ds(i * step, step), :],
            weights_ref[:, at],
            NN,
            preferred_element_type=F32,
        )
        part = (part * scale_ref[:, at]).astype(BF16)
        one, two = part[:, :width], part[:, width:]
        outs[0][pl.ds(i * step, step), :] = jnp.where(fast, one, two)
        outs[1][pl.ds(i * step, step), :] = jnp.where(fast, two, one)
    extra = outs[0].shape[0] - height
    if extra:
        masses = [mass_ref[:, pl.ds((2 * chunk + k) * width, width)] for k in range(2)]
        one, two = (high_low(mass, extra) for mass in masses)
        outs[0][pl.ds(height, extra), :] = jnp.where(fast, one, two)
        outs[1][pl.ds(height, extra), :] = jnp.where(fast, two, one)


def total_of(refs, height):
    total = refs[0][0:height, :].astype(F32)
    for ref in refs[1:]:
        total = total + ref[0:height, :].astype(F32)
    return total


def mass_of(refs, height):
    mass = 0.0
    for ref in refs:
        lines = ref[height : height + 16, :].astype(F32)
        mass = mass + (lines[0:1] + lines[1:2])
    return mass


def combine_kernel(*refs, height):
    out_ref = refs[-1]
    extra = out_ref.shape[0] - height
    out_ref[0:height, :] = total_of(refs[:-1], height).astype(BF16)
    if extra:
        out_ref[height : height + extra, :] = high_low(mass_of(refs[:-1], height), extra)


def finish_kernel(*refs, heights):
    out_ref, mass_ref = refs[-2:]
    terms = refs[:-2]
    mass = mass_of(terms[-2:], heights[-1])
    mass_ref[...] = mass
    inverse = 1.0 / mass
    start = 0
    for j, height in enumerate(heights):
        total = total_of(terms[2 * j : 2 * j + 2], height)
        out_ref[:, pl.ds(start, height)] = (total * inverse).T
        start += height


def body(embeddings, level_one, centroids):
    groups, peers = lax.axis_size("grp"), lax.axis_size("dev")
    routes = Routes(groups, peers)
    ring = routes.ring
    count, depth = embeddings.shape
    capacity = 2 * count // groups
    slots = groups * capacity
    owned = centroids.shape[0]
    clusters = owned * peers
    parts = 2

    own = call(
        unit_kernel,
        (shape(owned // parts, depth),) * parts,
        [send(centroids, routes.swap)],
        name="unit_centroids",
        cost_estimate=WAIT,
    )
    mine = [own]
    for s in range(1, ring):
        mine.append([send(p, routes.shift[1]) for p in mine[-1]])
    other = [[send(p, routes.core) for p in m] for m in mine]

    place = call(
        rank_kernel,
        shape(-(-groups // 8) * 8, count, dtype=jnp.int32),
        [level_one.reshape(1, count)],
        name="rank_rows",
    )

    def pick(d, after=()):
        return call(
            functools.partial(pick_kernel, which=d),
            shape(capacity, depth),
            [place, embeddings],
            after=after,
            name="pick_rows",
        )

    arrived, packed = {}, ()
    for d in [*range(2, groups), 1, 0]:
        packed = (pick(d, packed),)
        arrived[d] = send(packed[0], routes.cluster[d]) if d else packed[0]

    state_shapes = (
        shape(slots, depth),
        shape(1, slots, dtype=F32),
        shape(slots, clusters),
        shape(1, clusters, dtype=F32),
    )

    def absorb(state, raw, lines, columns):
        pieces = [p for s in columns for part in (mine, other) for p in part[s]]
        rows = [arrived[d] for d in raw]
        return call(
            functools.partial(
                weights_kernel,
                raw=raw,
                lines=lines,
                columns=columns,
                carried=bool(state),
                groups=groups,
            ),
            state_shapes,
            [*state, *rows, *pieces],
            alias={j: j for j in range(len(state))},
            name="weights",
        )

    early = list(range(ring - 1))
    state = absorb((), [0], [0], early)
    rest = list(range(1, groups))
    waited = rest
    arrived.update(zip(waited, tie([arrived[d] for d in waited], ())))
    state = absorb(state, rest, rest, early)
    rows, valid, weights, part = absorb(state, [], [0, *rest], [ring - 1])
    turned = call(
        turn_kernel, shape(depth, slots), [arrived[d] for d in range(groups)], name="turn_rows"
    )

    def sweep(part, last):
        chip = call(
            join_kernel,
            shape(1, clusters, dtype=F32),
            [part, send(part, routes.core)],
            name="join_cores",
        )
        near = [send(chip, routes.both[t]) for t in range(1, ring // 2)]
        totals = [chip, send(chip, routes.shift[ring // 2])]
        for value in near:
            totals += [value, send(value, routes.core)]
        outs = (shape(1, clusters, dtype=F32),)
        if last:
            outs += (shape(1, slots, dtype=F32), shape(1, clusters, dtype=F32))
        return call(
            functools.partial(sweep_kernel, ring=ring, last=last),
            outs,
            [valid, weights, *totals],
            scratch_shapes=() if last else (pltpu.VMEM((1, clusters), F32),),
            name="last_sweep" if last else "sweep",
        )

    for _ in range(SWEEPS - 1):
        (part,) = sweep(part, last=False)
    mass_part, row_scale, column_scale = sweep(part, last=True)

    heights = [depth * 4 // 8, depth - depth * 4 // 8]
    starts = [0, heights[0]]
    tall = [heights[0], heights[1] + 16]

    def numerator(s, j, after):
        fresh = scaled[j] is None
        args = [turned, weights, row_scale] if fresh else [scaled[j], weights]
        args = [*args, column_scale, mass_part]
        outs = (shape(tall[j], owned),) * 2
        if fresh:
            outs = (shape(heights[j], slots), *outs)
        outs = call(
            functools.partial(
                numerator_kernel, chunk=s, first=starts[j], height=heights[j], fresh=fresh
            ),
            outs,
            args,
            after=after,
            name="numerator",
            cost_estimate=cost(heights[j], 2 * owned, slots),
        )
        if fresh:
            scaled[j] = outs[0]
        return outs[-2], outs[-1]

    def combine(j, terms, after=()):
        return call(
            functools.partial(combine_kernel, height=heights[j]),
            shape(tall[j], owned),
            terms,
            after=after,
            name="combine",
            cost_estimate=BRIEF if j else TURN,
        )

    scaled = [None] * parts
    first, *others = [*range(1, ring), 0]
    pairs, moving, kept = {}, [()] * parts, [()] * parts

    def sums_of(s, after):
        for j in range(parts):
            kept_part, sent_part = numerator(s, j, after)
            pairs[s, j] = (kept_part, send(sent_part, routes.core))
            if s == first:
                after = (kept_part,)

    def step(s, after):
        route = routes.home if s == ring - 1 else routes.shift[1]
        made = []
        for j in range(parts):
            added = combine(j, (*moving[j], *pairs[s, j]), after)
            moving[j] = (send(added, route),)
            made.append(added)
            if s != first:
                after = (added,)
        return tuple(made)

    sums_of(first, ())
    after = step(first, ())
    for s in others:
        sums_of(s, after)
    after = tuple(pairs[s, j][0] for s in others for j in range(parts))
    for s in others[:-1]:
        after = step(s, after)
        if s == others[0]:
            for j in range(parts):
                kept[j] = send(combine(j, pairs[0, j], after), routes.swap)

    (arrived_first,) = tie(moving[0], (), TURN)
    moving[0] = (arrived_first,)
    updated, mass = call(
        functools.partial(finish_kernel, heights=heights),
        (shape(owned, depth, dtype=F32), shape(1, owned, dtype=F32)),
        [t for j in range(parts) for t in (moving[j][0], kept[j])],
        name="finish",
    )
    return updated, mass.reshape(owned)


def solution(mesh):
    in_specs = (P(AXES, None), P(AXES, None), P(AXES, None))
    out_specs = (P(AXES, None), P(AXES))
    return jax.shard_map(body, mesh=mesh, in_specs=in_specs, out_specs=out_specs, check_vma=False)
```

```python
import functools
import math

import jax
import jax.numpy as jnp
from jax import lax
from jax.experimental import pallas as pl
from jax.experimental.pallas import tpu as pltpu
from jax.sharding import PartitionSpec as P

SWEEPS = 3
EMPTY = 64.0
AXES = ("grp", "dev")
F32 = jnp.float32
BF16 = jnp.bfloat16
NT = (((1,), (1,)), ((), ()))
NN = (((1,), (0,)), ((), ()))
VMEM = pl.BlockSpec(memory_space=pltpu.VMEM)
SMEM = pl.BlockSpec(memory_space=pltpu.SMEM)
HELD = pl.BlockSpec(memory_space=pl.ANY)
PARAMS = pltpu.CompilerParams(vmem_limit_bytes=16 * 1024 * 1024)


def permutation(groups, peers, move):
    pairs = []
    for grp in range(groups):
        for dev in range(peers):
            target = move(grp // 2, grp % 2, dev // 2, dev % 2)
            if target is None:
                continue
            pair, side, place, half = target
            pairs.append((grp * peers + dev, (2 * pair + side) * peers + 2 * place + half))
    return pairs


class Routes:
    def __init__(self, groups, peers):
        self.ring = peers // 2
        make = functools.partial(permutation, groups, peers)
        turn = self.ring
        self.swap = make(lambda p, s, z, h: (p, h, z, s))
        self.core = make(lambda p, s, z, h: (p, 1 - s, z, h))
        self.shift = [make(lambda p, s, z, h, t=t: (p, s, (z + t) % turn, h)) for t in range(turn)]
        self.swap = make(lambda p, s, z, h: (p, h, z, s))
        self.both = [
            make(lambda p, s, z, h, t=t: (p, s, (z + (-t if s else t)) % turn, h))
            for t in range(turn // 2 + 1)
        ]
        self.home = make(lambda p, s, z, h: (p, h, (z + 1) % turn, s))
        self.cluster = [
            make(lambda p, s, z, h, d=d: ((2 * p + h ^ d) // 2, s, z, (2 * p + h ^ d) % 2))
            for d in range(groups)
        ]


def send(value, route):
    return lax.ppermute(value, AXES, route)


BRIEF = pl.CostEstimate(flops=1, bytes_accessed=1, transcendentals=0)
TURN = pl.CostEstimate(flops=6 * 10**9, bytes_accessed=1, transcendentals=0)
HALF = pl.CostEstimate(flops=4 * 10**9, bytes_accessed=1, transcendentals=0)
WAIT = pl.CostEstimate(flops=2 * 10**10, bytes_accessed=0, transcendentals=0)


def call(kernel, outs, args, after=(), specs=None, alias=None, out_specs=None, **kwargs):
    args, after = list(args), list(after)

    def ordered(*refs):
        kernel(*refs[: len(args)], *refs[len(args) + len(after) :])

    return pl.pallas_call(
        ordered,
        out_shape=outs,
        in_specs=(specs or [VMEM] * len(args)) + [HELD] * len(after),
        out_specs=out_specs or jax.tree.map(lambda _: VMEM, outs),
        input_output_aliases=alias or {},
        compiler_params=PARAMS,
        **kwargs,
    )(*args, *after)


def cost(m, n, k):
    return pl.CostEstimate(
        flops=2 * m * n * k, bytes_accessed=2 * (m * n + n * k + m * k), transcendentals=0
    )


def tie(values, after, hint=WAIT):
    values, after = list(values), list(after)
    return pl.pallas_call(
        lambda *refs: None,
        out_shape=tuple(jax.ShapeDtypeStruct(v.shape, v.dtype) for v in values),
        in_specs=[HELD] * (len(values) + len(after)),
        out_specs=(HELD,) * len(values),
        input_output_aliases={j: j for j in range(len(values))},
        compiler_params=PARAMS,
        cost_estimate=hint,
        name="tie",
    )(*values, *after)


def shape(*dims, dtype=BF16):
    return jax.ShapeDtypeStruct(dims, dtype)


def exact(line):
    high = line.astype(BF16).astype(F32)
    middle = (line - high).astype(BF16).astype(F32)
    low = line - high - middle
    at = lax.broadcasted_iota(jnp.int32, (16, line.shape[1]), 0)
    split = jnp.where(at == 0, high, jnp.where(at == 1, middle, jnp.where(at == 2, low, 0.0)))
    return split.astype(BF16)


def fast_here():
    return lax.axis_index("grp") % 2 == lax.axis_index("dev") % 2


def cluster_here():
    return lax.axis_index("grp") // 2 * 2 + lax.axis_index("dev") % 2


def unit(rows):
    wide = rows.astype(F32)
    inverse = lax.rsqrt(jnp.mean(wide * wide, axis=-1, keepdims=True) + 1e-06)
    return (wide * inverse).astype(BF16)


def unit_kernel(rows_ref, *outs):
    height = outs[0].shape[0]
    for j, out_ref in enumerate(outs):
        out_ref[...] = unit(rows_ref[pl.ds(j * height, height), :])


def rank_kernel(level_ref, place_ref):
    lines, count = place_ref.shape
    relative = level_ref[...] ^ cluster_here()
    member = lax.broadcasted_iota(jnp.int32, (lines, count), 0) == relative
    upto = lax.broadcasted_iota(jnp.int32, (count, count), 0) <= lax.broadcasted_iota(
        jnp.int32, (count, count), 1
    )
    running = lax.dot_general(
        member.astype(F32).astype(BF16),
        upto.astype(F32).astype(BF16),
        NN,
        preferred_element_type=F32,
    )
    place_ref[...] = jnp.where(member, running.astype(jnp.int32) - 1, -1)


def pick_kernel(place_ref, rows_ref, out_ref, *, which):
    capacity, count = out_ref.shape[0], rows_ref.shape[0]
    slots = lax.broadcasted_iota(jnp.int32, (capacity, count), 0)
    pick = (slots == place_ref[which : which + 1, :]).astype(F32)
    filled = jnp.sum(pick, axis=1, keepdims=True)
    picked = lax.dot_general(pick.astype(BF16), rows_ref[...], NN, preferred_element_type=F32)
    out_ref[...] = (picked + (1.0 - filled) * EMPTY).astype(BF16)


def weights_kernel(*refs, raw, lines, columns, carried, groups):
    *refs, unit_ref, valid_ref, weights_ref, sums_ref = refs
    inputs = refs[4 if carried else 0 :]
    pieces = inputs[len(raw) :]
    each = len(pieces) // (2 * len(columns))
    height = pieces[0].shape[0]
    capacity, depth = unit_ref.shape[0] // groups, unit_ref.shape[1]
    pick = lax.broadcasted_iota(jnp.int32, (16, 128), 0) + lax.broadcasted_iota(
        jnp.int32, (16, 128), 1
    )
    pick = jnp.where(pick == 0, 1.0, 0.0).astype(BF16)
    for ref, d in zip(inputs, raw):
        span = pl.ds(d * capacity, capacity)
        rows = ref[...]
        present = (rows[:, 0:1].astype(F32) < 0.5 * EMPTY).astype(F32)
        unit_ref[span, :] = unit(rows.astype(F32) * present)
        across = jnp.broadcast_to(present, (capacity, 128)).astype(BF16)
        valid = lax.dot_general(pick, across, NT, preferred_element_type=F32)
        valid_ref[:, span] = valid[0:1]

    fast = fast_here()
    half = each * height
    group = max(1, 512 // (2 * half))
    factor = 3.0 / math.sqrt(depth) * math.log2(math.e)
    for j in range(0, len(columns), group):
        block = []
        for k in range(j, min(j + group, len(columns))):
            refs = pieces[2 * each * k : 2 * each * (k + 1)]
            mine, other = (
                jnp.concatenate([ref[...] for ref in part], axis=0)
                for part in (refs[:each], refs[each:])
            )
            block += [jnp.where(fast, mine, other), jnp.where(fast, other, mine)]
        block = jnp.concatenate(block, axis=0)
        at = pl.ds(columns[j] * 2 * half, block.shape[0])
        for d in lines:
            span = pl.ds(d * capacity, capacity)
            scores = lax.dot_general(unit_ref[span, :], block, NT, preferred_element_type=F32)
            weights_ref[span, at] = jnp.exp2(scores * factor).astype(BF16)
    at = pl.ds(columns[0] * 2 * half, len(columns) * 2 * half)
    span = pl.ds(lines[0] * capacity, len(lines) * capacity)
    valid = jnp.broadcast_to(valid_ref[:, span], (16, len(lines) * capacity)).astype(BF16)
    sums = lax.dot_general(valid, weights_ref[span, at], NN, preferred_element_type=F32)[0:1]
    sums_ref[:, at] = sums if 0 in lines else sums_ref[:, at] + sums


def turn_kernel(*refs):
    rows, out_ref = refs[:-1], refs[-1]
    width = 2 * rows[0].shape[0]
    for j in range(len(rows) // 2):
        both = jnp.concatenate([rows[2 * j][...], rows[2 * j + 1][...]], axis=0)
        out_ref[:, pl.ds(j * width, width)] = both.T


def join_kernel(part_ref, other_ref, out_ref):
    out_ref[...] = part_ref[...] + other_ref[...]


def inverse_totals(totals, scale_ref):
    ring, width = len(totals), totals[0].shape[1] // len(totals)
    zero = lax.axis_index("grp") % 2 == 0
    for s in range(ring):

        def chunk(ref, t):
            return ref[:, pl.ds((s - t) % ring * width, width)]

        total = chunk(totals[0], 0) + chunk(totals[1], ring // 2)
        for t in range(1, ring // 2):
            near, far = totals[2 * t], totals[2 * t + 1]
            ahead = jnp.where(zero, chunk(near, t), chunk(far, t))
            behind = jnp.where(zero, chunk(far, -t), chunk(near, -t))
            total = total + (ahead + behind)
        scale_ref[:, pl.ds(s * width, width)] = 1.0 / total


def sweep_kernel(*refs, ring, last):
    valid_ref, weights_ref, *refs = refs
    totals = refs[:ring]
    if last:
        rows_ref, scale_ref = refs[ring:]
    else:
        out_ref, scale_ref = refs[ring:]
    inverse_totals(totals, scale_ref)
    weights, valid = weights_ref[...], valid_ref[...]
    total = lax.dot_general(exact(scale_ref[...]), weights, NT, preferred_element_type=F32)
    total = jnp.sum(total, axis=0, keepdims=True)
    row_scale = valid / (total + 1.0 - valid)
    if last:
        rows_ref[...] = row_scale
    else:
        out_ref[...] = column_sums(row_scale, weights)


def column_sums(row_scale, weights):
    sums = lax.dot_general(exact(row_scale), weights, NN, preferred_element_type=F32)
    return jnp.sum(sums, axis=0, keepdims=True)


def mass_kernel(rows_ref, scale_ref, weights_ref, out_ref):
    out_ref[...] = column_sums(rows_ref[...], weights_ref[...]) * scale_ref[...]


def high_low(total, height):
    line = lax.broadcasted_iota(jnp.int32, (height, total.shape[1]), 0)
    high = total.astype(BF16).astype(F32)
    return jnp.where(line == 0, high, jnp.where(line == 1, total - high, 0.0)).astype(BF16)


def numerator_kernel(turned_ref, weights_ref, *refs, chunk, first, height, fresh, extra):
    fast = fast_here()
    if fresh:
        rows_ref, scale_ref, *refs = refs
        *refs, scaled_ref, one_ref, two_ref = refs
        scaled = turned_ref[pl.ds(first, height), :].astype(F32) * rows_ref[...]
        scaled_ref[...] = scaled.astype(BF16)
    else:
        scale_ref, *refs, one_ref, two_ref = refs
        scaled_ref = turned_ref
    outs = (one_ref, two_ref)
    width = outs[0].shape[1]
    step = height if height <= 384 else height // 2
    at = pl.ds(chunk * 2 * width, 2 * width)
    for i in range(height // step):
        part = lax.dot_general(
            scaled_ref[pl.ds(i * step, step), :],
            weights_ref[:, at],
            NN,
            preferred_element_type=F32,
        )
        part = (part * scale_ref[:, at]).astype(BF16)
        one, two = part[:, :width], part[:, width:]
        outs[0][pl.ds(i * step, step), :] = jnp.where(fast, one, two)
        outs[1][pl.ds(i * step, step), :] = jnp.where(fast, two, one)
    if extra:
        (mass_ref,) = refs
        masses = [mass_ref[:, pl.ds((2 * chunk + k) * width, width)] for k in range(2)]
        one, two = (high_low(mass, extra) for mass in masses)
        outs[0][pl.ds(height, extra), :] = jnp.where(fast, one, two)
        outs[1][pl.ds(height, extra), :] = jnp.where(fast, two, one)


def total_of(refs, height):
    total = refs[0][0:height, :].astype(F32)
    for ref in refs[1:]:
        total = total + ref[0:height, :].astype(F32)
    return total


def mass_of(refs, height):
    mass = 0.0
    for ref in refs:
        lines = ref[height : height + 16, :].astype(F32)
        mass = mass + (lines[0:1] + lines[1:2])
    return mass


def combine_kernel(*refs, height):
    out_ref = refs[-1]
    extra = out_ref.shape[0] - height
    out_ref[0:height, :] = total_of(refs[:-1], height).astype(BF16)
    if extra:
        out_ref[height : height + extra, :] = high_low(mass_of(refs[:-1], height), extra)


def finish_kernel(*refs, heights):
    out_ref, mass_ref = refs[-2:]
    terms = refs[:-2]
    mass = mass_of(terms[-2:], heights[-1])
    mass_ref[...] = mass
    inverse = 1.0 / mass
    start = 0
    for j, height in enumerate(heights):
        total = total_of(terms[2 * j : 2 * j + 2], height)
        out_ref[:, pl.ds(start, height)] = (total * inverse).T
        start += height


def body(embeddings, level_one, centroids):
    groups, peers = lax.axis_size("grp"), lax.axis_size("dev")
    routes = Routes(groups, peers)
    ring = routes.ring
    count, depth = embeddings.shape
    capacity = 2 * count // groups
    slots = groups * capacity
    owned = centroids.shape[0]
    clusters = owned * peers
    parts = 2

    swapped = send(centroids, routes.swap)

    place = call(
        rank_kernel,
        shape(-(-groups // 8) * 8, count, dtype=jnp.int32),
        [level_one.reshape(1, count)],
        name="rank_rows",
    )

    def pick(d, after=()):
        return call(
            functools.partial(pick_kernel, which=d),
            shape(capacity, depth),
            [place, embeddings],
            after=after,
            name="pick_rows",
        )

    direct = list(range(groups // 2, 0, -1))
    distant = list(range(groups // 2 + 1, groups))
    packed = {}
    for d in [*direct, *distant, 0]:
        packed[d] = pick(d, tuple(packed.values())[-1:])
    arrived = {d: send(packed[d], routes.cluster[d]) for d in direct}

    own = call(
        unit_kernel,
        (shape(owned // parts, depth),) * parts,
        [swapped],
        after=[packed[0]],
        name="unit_centroids",
        cost_estimate=WAIT,
    )
    mine = [own]
    for s in range(1, ring):
        one, two = (send(p, routes.shift[1]) for p in mine[-1])
        if s < ring - 1:
            (one,) = tie([one], (), HALF)
            (two,) = tie([two], (one,), BRIEF)
        mine.append([one, two])
    for s in range(ring - 2):
        mine[s] = [tie([p], (q,), BRIEF)[0] for p, q in zip(mine[s], mine[s + 1])]
    mine[-2] = [tie([mine[-2][0]], mine[-1][:1], BRIEF)[0], mine[-2][1]]
    other = [[send(p, routes.core) for p in m] for m in mine[:-1]]

    waiting = tie([packed[d] for d in distant], [arrived[d] for d in direct], BRIEF)
    arrived |= {d: send(p, routes.cluster[d]) for d, p in zip(distant, waiting)}
    arrived[0] = packed[0]

    state_shapes = (
        shape(slots, depth),
        shape(1, slots, dtype=F32),
        shape(slots, clusters),
        shape(1, clusters, dtype=F32),
    )

    def absorb(state, raw, lines, columns):
        pieces = [p for s in columns for part in (mine, other) for p in part[s]]
        rows = [arrived[d] for d in raw]
        return call(
            functools.partial(
                weights_kernel,
                raw=raw,
                lines=lines,
                columns=columns,
                carried=bool(state),
                groups=groups,
            ),
            state_shapes,
            [*state, *rows, *pieces],
            alias={j: j for j in range(len(state))},
            name="weights",
        )

    near, early = [0, *sorted(direct)], list(range(ring - 1))
    state = absorb((), near, near, early[:-1])
    state = absorb(state, [], near, early[-1:])
    one, two = mine[-1]
    (one,) = tie([one], state[1:2], HALF)
    arrived.update(zip(distant, tie([arrived[d] for d in distant], (), BRIEF)))
    state = absorb(state, distant, distant, early)
    (two,) = tie([two], (one, state[1]), BRIEF)
    mine[-1] = [one, two]
    other.append([send(p, routes.core) for p in mine[-1]])
    rows, valid, weights, part = absorb(state, [], list(range(groups)), [ring - 1])
    turned = call(
        turn_kernel, shape(depth, slots), [arrived[d] for d in range(groups)], name="turn_rows"
    )

    def sweep(part, last):
        chip = call(
            join_kernel,
            shape(1, clusters, dtype=F32),
            [part, send(part, routes.core)],
            name="join_cores",
        )
        near = [send(chip, routes.both[t]) for t in range(1, ring // 2)]
        totals = [chip, send(chip, routes.shift[ring // 2])]
        for value in near:
            totals += [value, send(value, routes.core)]
        outs = (shape(1, clusters, dtype=F32),)
        if last:
            outs = (shape(1, slots, dtype=F32), *outs)
        return call(
            functools.partial(sweep_kernel, ring=ring, last=last),
            outs,
            [valid, weights, *totals],
            scratch_shapes=() if last else (pltpu.VMEM((1, clusters), F32),),
            name="last_sweep" if last else "sweep",
        )

    for _ in range(SWEEPS - 1):
        (part,) = sweep(part, last=False)
    row_scale, column_scale = sweep(part, last=True)

    heights = [depth * 4 // 8, depth - depth * 4 // 8]
    starts = [0, heights[0]]
    tall = [heights[0], heights[1] + 16]

    masses = []

    def numerator(s, j, after):
        fresh = scaled[j] is None
        args = [turned, weights, row_scale] if fresh else [scaled[j], weights]
        args = [*args, column_scale]
        if tall[j] > heights[j]:
            if not masses:
                masses.append(
                    call(
                        mass_kernel,
                        shape(1, clusters, dtype=F32),
                        [row_scale, column_scale, weights],
                        after=after,
                        name="masses",
                    )
                )
            args += masses
        outs = (shape(tall[j], owned),) * 2
        if fresh:
            outs = (shape(heights[j], slots), *outs)
        outs = call(
            functools.partial(
                numerator_kernel,
                chunk=s,
                first=starts[j],
                height=heights[j],
                fresh=fresh,
                extra=tall[j] - heights[j],
            ),
            outs,
            args,
            after=after,
            name="numerator",
            cost_estimate=cost(heights[j], 2 * owned, slots),
        )
        if fresh:
            scaled[j] = outs[0]
        return outs[-2], outs[-1]

    def combine(j, terms, after=()):
        return call(
            functools.partial(combine_kernel, height=heights[j]),
            shape(tall[j], owned),
            terms,
            after=after,
            name="combine",
            cost_estimate=BRIEF if j else TURN,
        )

    scaled = [None] * parts
    first, *others = [*range(1, ring), 0]
    pairs, moving, kept = {}, [()] * parts, [()] * parts

    def sums_of(s, after):
        for j in range(parts):
            kept_part, sent_part = numerator(s, j, after)
            pairs[s, j] = (kept_part, send(sent_part, routes.core))
            if s == first:
                after = (kept_part,)

    def step(s, after):
        route = routes.home if s == ring - 1 else routes.shift[1]
        sent = []
        for j in range(parts):
            added = combine(j, (*moving[j], *pairs[s, j]), after)
            moving[j] = (send(added, route),)
            sent.append(added)
            if s != first:
                after = (added,)
        return tuple(sent)

    sums_of(first, ())
    after = step(first, ())
    for s in others:
        sums_of(s, after)
    after = tuple(pairs[s, j][0] for s in others for j in range(parts))
    for s in others[:-1]:
        after = step(s, after)
        if s == others[0]:
            for j in range(parts):
                kept[j] = send(combine(j, pairs[0, j], after), routes.swap)

    (arrived_first,) = tie(moving[0], (), TURN)
    moving[0] = (arrived_first,)
    updated, mass = call(
        functools.partial(finish_kernel, heights=heights),
        (shape(owned, depth, dtype=F32), shape(1, owned, dtype=F32)),
        [t for j in range(parts) for t in (moving[j][0], kept[j])],
        name="finish",
    )
    return updated, mass.reshape(owned)


def solution(mesh):
    in_specs = (P(AXES, None), P(AXES, None), P(AXES, None))
    out_specs = (P(AXES, None), P(AXES))
    return jax.shard_map(body, mesh=mesh, in_specs=in_specs, out_specs=out_specs, check_vma=False)
```

```python
import functools
import math

import jax
import jax.numpy as jnp
from jax import lax
from jax.experimental import pallas as pl
from jax.experimental.pallas import tpu as pltpu
from jax.sharding import PartitionSpec as P

SWEEPS = 3
EMPTY = 64.0
AXES = ("grp", "dev")
F32 = jnp.float32
BF16 = jnp.bfloat16
NT = (((1,), (1,)), ((), ()))
NN = (((1,), (0,)), ((), ()))
VMEM = pl.BlockSpec(memory_space=pltpu.VMEM)
SMEM = pl.BlockSpec(memory_space=pltpu.SMEM)
HELD = pl.BlockSpec(memory_space=pl.ANY)
PARAMS = pltpu.CompilerParams(vmem_limit_bytes=16 * 1024 * 1024)


def permutation(groups, peers, move):
    pairs = []
    for grp in range(groups):
        for dev in range(peers):
            target = move(grp // 2, grp % 2, dev // 2, dev % 2)
            if target is None:
                continue
            pair, side, place, half = target
            pairs.append((grp * peers + dev, (2 * pair + side) * peers + 2 * place + half))
    return pairs


class Routes:
    def __init__(self, groups, peers):
        self.ring = peers // 2
        make = functools.partial(permutation, groups, peers)
        turn = self.ring
        self.swap = make(lambda p, s, z, h: (p, h, z, s))
        self.core = make(lambda p, s, z, h: (p, 1 - s, z, h))
        self.shift = [make(lambda p, s, z, h, t=t: (p, s, (z + t) % turn, h)) for t in range(turn)]
        self.swap = make(lambda p, s, z, h: (p, h, z, s))
        self.both = [
            make(lambda p, s, z, h, t=t: (p, s, (z + (-t if s else t)) % turn, h))
            for t in range(turn // 2 + 1)
        ]
        self.home = make(lambda p, s, z, h: (p, h, (z + 1) % turn, s))
        self.cluster = [
            make(lambda p, s, z, h, d=d: ((2 * p + h ^ d) // 2, s, z, (2 * p + h ^ d) % 2))
            for d in range(groups)
        ]


def send(value, route):
    return lax.ppermute(value, AXES, route)


BRIEF = pl.CostEstimate(flops=1, bytes_accessed=1, transcendentals=0)
TURN = pl.CostEstimate(flops=6 * 10**9, bytes_accessed=1, transcendentals=0)
HALF = pl.CostEstimate(flops=4 * 10**9, bytes_accessed=1, transcendentals=0)
WAIT = pl.CostEstimate(flops=2 * 10**10, bytes_accessed=0, transcendentals=0)


def call(kernel, outs, args, after=(), specs=None, alias=None, out_specs=None, **kwargs):
    args, after = list(args), list(after)

    def ordered(*refs):
        kernel(*refs[: len(args)], *refs[len(args) + len(after) :])

    return pl.pallas_call(
        ordered,
        out_shape=outs,
        in_specs=(specs or [VMEM] * len(args)) + [HELD] * len(after),
        out_specs=out_specs or jax.tree.map(lambda _: VMEM, outs),
        input_output_aliases=alias or {},
        compiler_params=PARAMS,
        **kwargs,
    )(*args, *after)


def cost(m, n, k):
    return pl.CostEstimate(
        flops=2 * m * n * k, bytes_accessed=2 * (m * n + n * k + m * k), transcendentals=0
    )


def tie(values, after, hint=WAIT):
    values, after = list(values), list(after)
    return pl.pallas_call(
        lambda *refs: None,
        out_shape=tuple(jax.ShapeDtypeStruct(v.shape, v.dtype) for v in values),
        in_specs=[HELD] * (len(values) + len(after)),
        out_specs=(HELD,) * len(values),
        input_output_aliases={j: j for j in range(len(values))},
        compiler_params=PARAMS,
        cost_estimate=hint,
        name="tie",
    )(*values, *after)


def shape(*dims, dtype=BF16):
    return jax.ShapeDtypeStruct(dims, dtype)


def exact(line):
    high = line.astype(BF16).astype(F32)
    middle = (line - high).astype(BF16).astype(F32)
    low = line - high - middle
    at = lax.broadcasted_iota(jnp.int32, (16, line.shape[1]), 0)
    split = jnp.where(at == 0, high, jnp.where(at == 1, middle, jnp.where(at == 2, low, 0.0)))
    return split.astype(BF16)


def fast_here():
    return lax.axis_index("grp") % 2 == lax.axis_index("dev") % 2


def cluster_here():
    return lax.axis_index("grp") // 2 * 2 + lax.axis_index("dev") % 2


def unit(rows):
    wide = rows.astype(F32)
    inverse = lax.rsqrt(jnp.mean(wide * wide, axis=-1, keepdims=True) + 1e-06)
    return (wide * inverse).astype(BF16)


def unit_kernel(rows_ref, *outs):
    start = 0
    for out_ref in outs:
        out_ref[...] = unit(rows_ref[pl.ds(start, out_ref.shape[0]), :])
        start += out_ref.shape[0]


def rank_kernel(level_ref, place_ref):
    lines, count = place_ref.shape
    relative = level_ref[...] ^ cluster_here()
    member = lax.broadcasted_iota(jnp.int32, (lines, count), 0) == relative
    upto = lax.broadcasted_iota(jnp.int32, (count, count), 0) <= lax.broadcasted_iota(
        jnp.int32, (count, count), 1
    )
    running = lax.dot_general(
        member.astype(F32).astype(BF16),
        upto.astype(F32).astype(BF16),
        NN,
        preferred_element_type=F32,
    )
    place_ref[...] = jnp.where(member, running.astype(jnp.int32) - 1, -1)


def pick_kernel(place_ref, rows_ref, out_ref, *, which):
    capacity, count = out_ref.shape[0], rows_ref.shape[0]
    slots = lax.broadcasted_iota(jnp.int32, (capacity, count), 0)
    pick = (slots == place_ref[which : which + 1, :]).astype(F32)
    filled = jnp.sum(pick, axis=1, keepdims=True)
    picked = lax.dot_general(pick.astype(BF16), rows_ref[...], NN, preferred_element_type=F32)
    out_ref[...] = (picked + (1.0 - filled) * EMPTY).astype(BF16)


def weights_kernel(*refs, raw, lines, columns, carried, groups):
    *refs, unit_ref, valid_ref, weights_ref, sums_ref = refs
    inputs = refs[4 if carried else 0 :]
    pieces = inputs[len(raw) :]
    each = len(pieces) // (2 * len(columns))
    height = sum(p.shape[0] for p in pieces[:each]) // each
    capacity, depth = unit_ref.shape[0] // groups, unit_ref.shape[1]
    pick = lax.broadcasted_iota(jnp.int32, (16, 128), 0) + lax.broadcasted_iota(
        jnp.int32, (16, 128), 1
    )
    pick = jnp.where(pick == 0, 1.0, 0.0).astype(BF16)
    for ref, d in zip(inputs, raw):
        span = pl.ds(d * capacity, capacity)
        rows = ref[...]
        present = (rows[:, 0:1].astype(F32) < 0.5 * EMPTY).astype(F32)
        unit_ref[span, :] = unit(rows.astype(F32) * present)
        across = jnp.broadcast_to(present, (capacity, 128)).astype(BF16)
        valid = lax.dot_general(pick, across, NT, preferred_element_type=F32)
        valid_ref[:, span] = valid[0:1]

    fast = fast_here()
    half = each * height
    group = max(1, 512 // (2 * half))
    factor = 3.0 / math.sqrt(depth) * math.log2(math.e)
    for j in range(0, len(columns), group):
        block = []
        for k in range(j, min(j + group, len(columns))):
            refs = pieces[2 * each * k : 2 * each * (k + 1)]
            mine, other = (
                jnp.concatenate([ref[...] for ref in part], axis=0)
                for part in (refs[:each], refs[each:])
            )
            block += [jnp.where(fast, mine, other), jnp.where(fast, other, mine)]
        block = jnp.concatenate(block, axis=0)
        at = pl.ds(columns[j] * 2 * half, block.shape[0])
        for d in lines:
            span = pl.ds(d * capacity, capacity)
            scores = lax.dot_general(unit_ref[span, :], block, NT, preferred_element_type=F32)
            weights_ref[span, at] = jnp.exp2(scores * factor).astype(BF16)
    at = pl.ds(columns[0] * 2 * half, len(columns) * 2 * half)
    span = pl.ds(lines[0] * capacity, len(lines) * capacity)
    valid = jnp.broadcast_to(valid_ref[:, span], (16, len(lines) * capacity)).astype(BF16)
    sums = lax.dot_general(valid, weights_ref[span, at], NN, preferred_element_type=F32)[0:1]
    sums_ref[:, at] = sums if 0 in lines else sums_ref[:, at] + sums


def turn_kernel(*refs):
    rows, out_ref = refs[:-1], refs[-1]
    width = 2 * rows[0].shape[0]
    for j in range(len(rows) // 2):
        both = jnp.concatenate([rows[2 * j][...], rows[2 * j + 1][...]], axis=0)
        out_ref[:, pl.ds(j * width, width)] = both.T


def join_kernel(part_ref, other_ref, out_ref):
    out_ref[...] = part_ref[...] + other_ref[...]


def inverse_totals(totals, scale_ref):
    ring, width = len(totals), totals[0].shape[1] // len(totals)
    zero = lax.axis_index("grp") % 2 == 0
    for s in range(ring):

        def chunk(ref, t):
            return ref[:, pl.ds((s - t) % ring * width, width)]

        total = chunk(totals[0], 0) + chunk(totals[1], ring // 2)
        for t in range(1, ring // 2):
            near, far = totals[2 * t], totals[2 * t + 1]
            ahead = jnp.where(zero, chunk(near, t), chunk(far, t))
            behind = jnp.where(zero, chunk(far, -t), chunk(near, -t))
            total = total + (ahead + behind)
        scale_ref[:, pl.ds(s * width, width)] = 1.0 / total


def sweep_kernel(*refs, ring, last):
    valid_ref, weights_ref, *refs = refs
    totals = refs[:ring]
    if last:
        rows_ref, scale_ref = refs[ring:]
    else:
        out_ref, scale_ref = refs[ring:]
    inverse_totals(totals, scale_ref)
    weights, valid = weights_ref[...], valid_ref[...]
    total = lax.dot_general(exact(scale_ref[...]), weights, NT, preferred_element_type=F32)
    total = jnp.sum(total, axis=0, keepdims=True)
    row_scale = valid / (total + 1.0 - valid)
    if last:
        rows_ref[...] = row_scale
    else:
        out_ref[...] = column_sums(row_scale, weights)


def column_sums(row_scale, weights):
    sums = lax.dot_general(exact(row_scale), weights, NN, preferred_element_type=F32)
    return jnp.sum(sums, axis=0, keepdims=True)


def mass_kernel(rows_ref, scale_ref, weights_ref, out_ref):
    out_ref[...] = column_sums(rows_ref[...], weights_ref[...]) * scale_ref[...]


def high_low(total, height):
    line = lax.broadcasted_iota(jnp.int32, (height, total.shape[1]), 0)
    high = total.astype(BF16).astype(F32)
    return jnp.where(line == 0, high, jnp.where(line == 1, total - high, 0.0)).astype(BF16)


def numerator_kernel(turned_ref, weights_ref, *refs, chunk, first, height, fresh, extra):
    fast = fast_here()
    if fresh:
        rows_ref, scale_ref, *refs = refs
        *refs, scaled_ref, one_ref, two_ref = refs
        scaled = turned_ref[pl.ds(first, height), :].astype(F32) * rows_ref[...]
        scaled_ref[...] = scaled.astype(BF16)
    else:
        scale_ref, *refs, one_ref, two_ref = refs
        scaled_ref = turned_ref
    outs = (one_ref, two_ref)
    width = outs[0].shape[1]
    step = height if height <= 384 else height // 2
    at = pl.ds(chunk * 2 * width, 2 * width)
    for i in range(height // step):
        part = lax.dot_general(
            scaled_ref[pl.ds(i * step, step), :],
            weights_ref[:, at],
            NN,
            preferred_element_type=F32,
        )
        part = (part * scale_ref[:, at]).astype(BF16)
        one, two = part[:, :width], part[:, width:]
        outs[0][pl.ds(i * step, step), :] = jnp.where(fast, one, two)
        outs[1][pl.ds(i * step, step), :] = jnp.where(fast, two, one)
    if extra:
        (mass_ref,) = refs
        masses = [mass_ref[:, pl.ds((2 * chunk + k) * width, width)] for k in range(2)]
        one, two = (high_low(mass, extra) for mass in masses)
        outs[0][pl.ds(height, extra), :] = jnp.where(fast, one, two)
        outs[1][pl.ds(height, extra), :] = jnp.where(fast, two, one)


def total_of(refs, height):
    total = refs[0][0:height, :].astype(F32)
    for ref in refs[1:]:
        total = total + ref[0:height, :].astype(F32)
    return total


def mass_of(refs, height):
    mass = 0.0
    for ref in refs:
        lines = ref[height : height + 16, :].astype(F32)
        mass = mass + (lines[0:1] + lines[1:2])
    return mass


def combine_kernel(*refs, height):
    out_ref = refs[-1]
    extra = out_ref.shape[0] - height
    out_ref[0:height, :] = total_of(refs[:-1], height).astype(BF16)
    if extra:
        out_ref[height : height + extra, :] = high_low(mass_of(refs[:-1], height), extra)


def finish_kernel(*refs, heights):
    out_ref, mass_ref = refs[-2:]
    terms = refs[:-2]
    mass = mass_of(terms[-2:], heights[-1])
    mass_ref[...] = mass
    inverse = 1.0 / mass
    start = 0
    for j, height in enumerate(heights):
        total = total_of(terms[2 * j : 2 * j + 2], height)
        out_ref[:, pl.ds(start, height)] = (total * inverse).T
        start += height


def body(embeddings, level_one, centroids):
    groups, peers = lax.axis_size("grp"), lax.axis_size("dev")
    routes = Routes(groups, peers)
    ring = routes.ring
    count, depth = embeddings.shape
    capacity = 2 * count // groups
    slots = groups * capacity
    owned = centroids.shape[0]
    clusters = owned * peers
    parts = 2

    small = max(16, owned * 6 // 256 * 16)
    swapped = send(centroids, routes.swap)

    place = call(
        rank_kernel,
        shape(-(-groups // 8) * 8, count, dtype=jnp.int32),
        [level_one.reshape(1, count)],
        name="rank_rows",
    )

    def pick(d, after=()):
        return call(
            functools.partial(pick_kernel, which=d),
            shape(capacity, depth),
            [place, embeddings],
            after=after,
            name="pick_rows",
        )

    direct = list(range(groups // 2, 0, -1))
    distant = list(range(groups // 2 + 1, groups))
    packed = {}
    for d in [*direct, *distant, 0]:
        packed[d] = pick(d, tuple(packed.values())[-1:])
    arrived = {d: send(packed[d], routes.cluster[d]) for d in direct}

    own = call(
        unit_kernel,
        (shape(small, depth), shape(owned - small, depth)),
        [swapped],
        after=[packed[0]],
        name="unit_centroids",
        cost_estimate=WAIT,
    )
    mine = [own]
    for s in range(1, ring):
        one, two = (send(p, routes.shift[1]) for p in mine[-1])
        if s < ring - 1:
            (one,) = tie([one], (), HALF)
            (two,) = tie([two], (one,), BRIEF)
        mine.append([one, two])
    for s in range(ring - 2):
        mine[s] = [tie([p], (q,), BRIEF)[0] for p, q in zip(mine[s], mine[s + 1])]
    mine[-2] = [tie([mine[-2][0]], mine[-1][:1], BRIEF)[0], mine[-2][1]]
    other = [[send(p, routes.core) for p in m] for m in mine[:-1]]

    waiting = tie([packed[d] for d in distant], [arrived[d] for d in direct], BRIEF)
    arrived |= {d: send(p, routes.cluster[d]) for d, p in zip(distant, waiting)}
    arrived[0] = packed[0]

    state_shapes = (
        shape(slots, depth),
        shape(1, slots, dtype=F32),
        shape(slots, clusters),
        shape(1, clusters, dtype=F32),
    )

    def absorb(state, raw, lines, columns):
        pieces = [p for s in columns for part in (mine, other) for p in part[s]]
        rows = [arrived[d] for d in raw]
        return call(
            functools.partial(
                weights_kernel,
                raw=raw,
                lines=lines,
                columns=columns,
                carried=bool(state),
                groups=groups,
            ),
            state_shapes,
            [*state, *rows, *pieces],
            alias={j: j for j in range(len(state))},
            name="weights",
        )

    near, early = [0, *sorted(direct)], list(range(ring - 1))
    state = absorb((), near, near, early[:-1])
    state = absorb(state, [], near, early[-1:])
    one, two = mine[-1]
    (one,) = tie([one], state[1:2], HALF)
    arrived.update(zip(distant, tie([arrived[d] for d in distant], (), BRIEF)))
    state = absorb(state, distant, distant, early)
    (two,) = tie([two], (one, state[1]), BRIEF)
    mine[-1] = [one, two]
    other.append([send(p, routes.core) for p in mine[-1]])
    rows, valid, weights, part = absorb(state, [], list(range(groups)), [ring - 1])
    turned = call(
        turn_kernel, shape(depth, slots), [arrived[d] for d in range(groups)], name="turn_rows"
    )

    def sweep(part, last):
        chip = call(
            join_kernel,
            shape(1, clusters, dtype=F32),
            [part, send(part, routes.core)],
            name="join_cores",
        )
        near = [send(chip, routes.both[t]) for t in range(1, ring // 2)]
        totals = [chip, send(chip, routes.shift[ring // 2])]
        for value in near:
            totals += [value, send(value, routes.core)]
        outs = (shape(1, clusters, dtype=F32),)
        if last:
            outs = (shape(1, slots, dtype=F32), *outs)
        return call(
            functools.partial(sweep_kernel, ring=ring, last=last),
            outs,
            [valid, weights, *totals],
            scratch_shapes=() if last else (pltpu.VMEM((1, clusters), F32),),
            name="last_sweep" if last else "sweep",
        )

    for _ in range(SWEEPS - 1):
        (part,) = sweep(part, last=False)
    row_scale, column_scale = sweep(part, last=True)

    heights = [depth * 4 // 8, depth - depth * 4 // 8]
    starts = [0, heights[0]]
    tall = [heights[0], heights[1] + 16]

    masses = []

    def numerator(s, j, after):
        fresh = scaled[j] is None
        args = [turned, weights, row_scale] if fresh else [scaled[j], weights]
        args = [*args, column_scale]
        if tall[j] > heights[j]:
            if not masses:
                masses.append(
                    call(
                        mass_kernel,
                        shape(1, clusters, dtype=F32),
                        [row_scale, column_scale, weights],
                        after=after,
                        name="masses",
                    )
                )
            args += masses
        outs = (shape(tall[j], owned),) * 2
        if fresh:
            outs = (shape(heights[j], slots), *outs)
        outs = call(
            functools.partial(
                numerator_kernel,
                chunk=s,
                first=starts[j],
                height=heights[j],
                fresh=fresh,
                extra=tall[j] - heights[j],
            ),
            outs,
            args,
            after=after,
            name="numerator",
            cost_estimate=cost(heights[j], 2 * owned, slots),
        )
        if fresh:
            scaled[j] = outs[0]
        return outs[-2], outs[-1]

    def combine(j, terms, after=()):
        return call(
            functools.partial(combine_kernel, height=heights[j]),
            shape(tall[j], owned),
            terms,
            after=after,
            name="combine",
            cost_estimate=BRIEF if j else TURN,
        )

    scaled = [None] * parts
    first, *others = [*range(1, ring), 0]
    pairs, moving, kept = {}, [()] * parts, [()] * parts

    def sums_of(s, after):
        for j in range(parts):
            kept_part, sent_part = numerator(s, j, after)
            pairs[s, j] = (kept_part, send(sent_part, routes.core))
            if s == first:
                after = (kept_part,)

    def step(s, after):
        route = routes.home if s == ring - 1 else routes.shift[1]
        sent = []
        for j in range(parts):
            added = combine(j, (*moving[j], *pairs[s, j]), after)
            moving[j] = (send(added, route),)
            sent.append(added)
            if s != first:
                after = (added,)
        return tuple(sent)

    sums_of(first, ())
    after = step(first, ())
    for s in others:
        sums_of(s, after)
    after = tuple(pairs[s, j][0] for s in others for j in range(parts))
    for s in others[:-1]:
        after = step(s, after)
        if s == others[0]:
            for j in range(parts):
                kept[j] = send(combine(j, pairs[0, j], after), routes.swap)

    (arrived_first,) = tie(moving[0], (), TURN)
    moving[0] = (arrived_first,)
    updated, mass = call(
        functools.partial(finish_kernel, heights=heights),
        (shape(owned, depth, dtype=F32), shape(1, owned, dtype=F32)),
        [t for j in range(parts) for t in (moving[j][0], kept[j])],
        name="finish",
    )
    return updated, mass.reshape(owned)


def solution(mesh):
    in_specs = (P(AXES, None), P(AXES, None), P(AXES, None))
    out_specs = (P(AXES, None), P(AXES))
    return jax.shard_map(body, mesh=mesh, in_specs=in_specs, out_specs=out_specs, check_vma=False)
```

```python
import functools
import math

import jax
import jax.numpy as jnp
from jax import lax
from jax.experimental import pallas as pl
from jax.experimental.pallas import tpu as pltpu
from jax.sharding import PartitionSpec as P

SWEEPS = 3
EMPTY = 64.0
AXES = ("grp", "dev")
F32 = jnp.float32
BF16 = jnp.bfloat16
NT = (((1,), (1,)), ((), ()))
NN = (((1,), (0,)), ((), ()))
VMEM = pl.BlockSpec(memory_space=pltpu.VMEM)
SMEM = pl.BlockSpec(memory_space=pltpu.SMEM)
HELD = pl.BlockSpec(memory_space=pl.ANY)
PARAMS = pltpu.CompilerParams(vmem_limit_bytes=16 * 1024 * 1024)


def permutation(groups, peers, move):
    pairs = []
    for grp in range(groups):
        for dev in range(peers):
            target = move(grp // 2, grp % 2, dev // 2, dev % 2)
            if target is None:
                continue
            pair, side, place, half = target
            pairs.append((grp * peers + dev, (2 * pair + side) * peers + 2 * place + half))
    return pairs


class Routes:
    def __init__(self, groups, peers):
        self.ring = peers // 2
        make = functools.partial(permutation, groups, peers)
        turn = self.ring
        self.swap = make(lambda p, s, z, h: (p, h, z, s))
        self.core = make(lambda p, s, z, h: (p, 1 - s, z, h))
        self.shift = [make(lambda p, s, z, h, t=t: (p, s, (z + t) % turn, h)) for t in range(turn)]
        self.swap = make(lambda p, s, z, h: (p, h, z, s))
        self.both = [
            make(lambda p, s, z, h, t=t: (p, s, (z + (-t if s else t)) % turn, h))
            for t in range(turn // 2 + 1)
        ]
        self.home = make(lambda p, s, z, h: (p, h, (z + 1) % turn, s))
        self.cluster = [
            make(lambda p, s, z, h, d=d: ((2 * p + h ^ d) // 2, s, z, (2 * p + h ^ d) % 2))
            for d in range(groups)
        ]


def send(value, route):
    return lax.ppermute(value, AXES, route)


BRIEF = pl.CostEstimate(flops=1, bytes_accessed=1, transcendentals=0)
TURN = pl.CostEstimate(flops=6 * 10**9, bytes_accessed=1, transcendentals=0)
HALF = pl.CostEstimate(flops=4 * 10**9, bytes_accessed=1, transcendentals=0)
WAIT = pl.CostEstimate(flops=2 * 10**10, bytes_accessed=0, transcendentals=0)


def call(kernel, outs, args, after=(), specs=None, alias=None, out_specs=None, **kwargs):
    args, after = list(args), list(after)

    def ordered(*refs):
        kernel(*refs[: len(args)], *refs[len(args) + len(after) :])

    return pl.pallas_call(
        ordered,
        out_shape=outs,
        in_specs=(specs or [VMEM] * len(args)) + [HELD] * len(after),
        out_specs=out_specs or jax.tree.map(lambda _: VMEM, outs),
        input_output_aliases=alias or {},
        compiler_params=PARAMS,
        **kwargs,
    )(*args, *after)


def cost(m, n, k):
    return pl.CostEstimate(
        flops=2 * m * n * k, bytes_accessed=2 * (m * n + n * k + m * k), transcendentals=0
    )


def tie(values, after, hint=WAIT):
    values, after = list(values), list(after)
    return pl.pallas_call(
        lambda *refs: None,
        out_shape=tuple(jax.ShapeDtypeStruct(v.shape, v.dtype) for v in values),
        in_specs=[HELD] * (len(values) + len(after)),
        out_specs=(HELD,) * len(values),
        input_output_aliases={j: j for j in range(len(values))},
        compiler_params=PARAMS,
        cost_estimate=hint,
        name="tie",
    )(*values, *after)


def shape(*dims, dtype=BF16):
    return jax.ShapeDtypeStruct(dims, dtype)


def exact(line):
    high = line.astype(BF16).astype(F32)
    middle = (line - high).astype(BF16).astype(F32)
    low = line - high - middle
    at = lax.broadcasted_iota(jnp.int32, (16, line.shape[1]), 0)
    split = jnp.where(at == 0, high, jnp.where(at == 1, middle, jnp.where(at == 2, low, 0.0)))
    return split.astype(BF16)


def fast_here():
    return lax.axis_index("grp") % 2 == lax.axis_index("dev") % 2


def cluster_here():
    return lax.axis_index("grp") // 2 * 2 + lax.axis_index("dev") % 2


def unit(rows):
    wide = rows.astype(F32)
    inverse = lax.rsqrt(jnp.mean(wide * wide, axis=-1, keepdims=True) + 1e-06)
    return (wide * inverse).astype(BF16)


def unit_kernel(rows_ref, *outs):
    start = 0
    for out_ref in outs:
        out_ref[...] = unit(rows_ref[pl.ds(start, out_ref.shape[0]), :])
        start += out_ref.shape[0]


def rank_kernel(level_ref, place_ref):
    lines, count = place_ref.shape
    relative = level_ref[...] ^ cluster_here()
    member = lax.broadcasted_iota(jnp.int32, (lines, count), 0) == relative
    upto = lax.broadcasted_iota(jnp.int32, (count, count), 0) <= lax.broadcasted_iota(
        jnp.int32, (count, count), 1
    )
    running = lax.dot_general(
        member.astype(F32).astype(BF16),
        upto.astype(F32).astype(BF16),
        NN,
        preferred_element_type=F32,
    )
    place_ref[...] = jnp.where(member, running.astype(jnp.int32) - 1, -1)


def pick_kernel(place_ref, rows_ref, out_ref, *, which):
    capacity, count = out_ref.shape[0], rows_ref.shape[0]
    slots = lax.broadcasted_iota(jnp.int32, (capacity, count), 0)
    pick = (slots == place_ref[which : which + 1, :]).astype(F32)
    filled = jnp.sum(pick, axis=1, keepdims=True)
    picked = lax.dot_general(pick.astype(BF16), rows_ref[...], NN, preferred_element_type=F32)
    out_ref[...] = (picked + (1.0 - filled) * EMPTY).astype(BF16)


def weights_kernel(*refs, raw, lines, columns, carried, groups):
    *refs, unit_ref, valid_ref, weights_ref, sums_ref = refs
    inputs = refs[4 if carried else 0 :]
    pieces = inputs[len(raw) :]
    each = len(pieces) // (2 * len(columns))
    height = sum(p.shape[0] for p in pieces[:each]) // each
    capacity, depth = unit_ref.shape[0] // groups, unit_ref.shape[1]
    pick = lax.broadcasted_iota(jnp.int32, (16, 128), 0) + lax.broadcasted_iota(
        jnp.int32, (16, 128), 1
    )
    pick = jnp.where(pick == 0, 1.0, 0.0).astype(BF16)
    for ref, d in zip(inputs, raw):
        span = pl.ds(d * capacity, capacity)
        rows = ref[...]
        present = (rows[:, 0:1].astype(F32) < 0.5 * EMPTY).astype(F32)
        unit_ref[span, :] = unit(rows.astype(F32) * present)
        across = jnp.broadcast_to(present, (capacity, 128)).astype(BF16)
        valid = lax.dot_general(pick, across, NT, preferred_element_type=F32)
        valid_ref[:, span] = valid[0:1]

    fast = fast_here()
    half = each * height
    group = max(1, 512 // (2 * half))
    factor = 3.0 / math.sqrt(depth) * math.log2(math.e)
    for j in range(0, len(columns), group):
        block = []
        for k in range(j, min(j + group, len(columns))):
            refs = pieces[2 * each * k : 2 * each * (k + 1)]
            mine, other = (
                jnp.concatenate([ref[...] for ref in part], axis=0)
                for part in (refs[:each], refs[each:])
            )
            block += [jnp.where(fast, mine, other), jnp.where(fast, other, mine)]
        block = jnp.concatenate(block, axis=0)
        at = pl.ds(columns[j] * 2 * half, block.shape[0])
        for d in lines:
            span = pl.ds(d * capacity, capacity)
            scores = lax.dot_general(unit_ref[span, :], block, NT, preferred_element_type=F32)
            weights_ref[span, at] = jnp.exp2(scores * factor).astype(BF16)
    at = pl.ds(columns[0] * 2 * half, len(columns) * 2 * half)
    span = pl.ds(lines[0] * capacity, len(lines) * capacity)
    valid = jnp.broadcast_to(valid_ref[:, span], (16, len(lines) * capacity)).astype(BF16)
    sums = lax.dot_general(valid, weights_ref[span, at], NN, preferred_element_type=F32)[0:1]
    sums_ref[:, at] = sums if 0 in lines else sums_ref[:, at] + sums


def turn_kernel(*refs):
    rows, out_ref = refs[:-1], refs[-1]
    width = 2 * rows[0].shape[0]
    for j in range(len(rows) // 2):
        both = jnp.concatenate([rows[2 * j][...], rows[2 * j + 1][...]], axis=0)
        out_ref[:, pl.ds(j * width, width)] = both.T


def join_kernel(part_ref, other_ref, out_ref):
    out_ref[...] = part_ref[...] + other_ref[...]


def inverse_totals(totals, scale_ref):
    ring, width = len(totals), totals[0].shape[1] // len(totals)
    zero = lax.axis_index("grp") % 2 == 0
    for s in range(ring):

        def chunk(ref, t):
            return ref[:, pl.ds((s - t) % ring * width, width)]

        total = chunk(totals[0], 0) + chunk(totals[1], ring // 2)
        for t in range(1, ring // 2):
            near, far = totals[2 * t], totals[2 * t + 1]
            ahead = jnp.where(zero, chunk(near, t), chunk(far, t))
            behind = jnp.where(zero, chunk(far, -t), chunk(near, -t))
            total = total + (ahead + behind)
        scale_ref[:, pl.ds(s * width, width)] = 1.0 / total


def sweep_kernel(*refs, ring, last):
    valid_ref, weights_ref, *refs = refs
    totals = refs[:ring]
    if last:
        rows_ref, scale_ref = refs[ring:]
    else:
        out_ref, scale_ref = refs[ring:]
    inverse_totals(totals, scale_ref)
    weights, valid = weights_ref[...], valid_ref[...]
    total = lax.dot_general(exact(scale_ref[...]), weights, NT, preferred_element_type=F32)
    total = jnp.sum(total, axis=0, keepdims=True)
    row_scale = valid / (total + 1.0 - valid)
    if last:
        rows_ref[...] = row_scale
    else:
        out_ref[...] = column_sums(row_scale, weights)


def column_sums(row_scale, weights):
    sums = lax.dot_general(exact(row_scale), weights, NN, preferred_element_type=F32)
    return jnp.sum(sums, axis=0, keepdims=True)


def mass_kernel(rows_ref, scale_ref, weights_ref, out_ref):
    out_ref[...] = column_sums(rows_ref[...], weights_ref[...]) * scale_ref[...]


def high_low(total, height):
    line = lax.broadcasted_iota(jnp.int32, (height, total.shape[1]), 0)
    high = total.astype(BF16).astype(F32)
    return jnp.where(line == 0, high, jnp.where(line == 1, total - high, 0.0)).astype(BF16)


def numerator_kernel(turned_ref, weights_ref, *refs, chunk, first, height, fresh, extra):
    fast = fast_here()
    if fresh:
        rows_ref, scale_ref, *refs = refs
        *refs, scaled_ref, one_ref, two_ref = refs
        scaled = turned_ref[pl.ds(first, height), :].astype(F32) * rows_ref[...]
        scaled_ref[...] = scaled.astype(BF16)
    else:
        scale_ref, *refs, one_ref, two_ref = refs
        scaled_ref = turned_ref
    outs = (one_ref, two_ref)
    width = outs[0].shape[1]
    step = height if height <= 384 else height // 2
    at = pl.ds(chunk * 2 * width, 2 * width)
    for i in range(height // step):
        part = lax.dot_general(
            scaled_ref[pl.ds(i * step, step), :],
            weights_ref[:, at],
            NN,
            preferred_element_type=F32,
        )
        part = (part * scale_ref[:, at]).astype(BF16)
        one, two = part[:, :width], part[:, width:]
        outs[0][pl.ds(i * step, step), :] = jnp.where(fast, one, two)
        outs[1][pl.ds(i * step, step), :] = jnp.where(fast, two, one)
    if extra:
        (mass_ref,) = refs
        masses = [mass_ref[:, pl.ds((2 * chunk + k) * width, width)] for k in range(2)]
        one, two = (high_low(mass, extra) for mass in masses)
        outs[0][pl.ds(height, extra), :] = jnp.where(fast, one, two)
        outs[1][pl.ds(height, extra), :] = jnp.where(fast, two, one)


def total_of(refs, height):
    total = refs[0][0:height, :].astype(F32)
    for ref in refs[1:]:
        total = total + ref[0:height, :].astype(F32)
    return total


def mass_of(refs, height):
    mass = 0.0
    for ref in refs:
        lines = ref[height : height + 16, :].astype(F32)
        mass = mass + (lines[0:1] + lines[1:2])
    return mass


def combine_kernel(*refs, height):
    out_ref = refs[-1]
    extra = out_ref.shape[0] - height
    out_ref[0:height, :] = total_of(refs[:-1], height).astype(BF16)
    if extra:
        out_ref[height : height + extra, :] = high_low(mass_of(refs[:-1], height), extra)


def finish_kernel(*refs, heights):
    out_ref, mass_ref = refs[-2:]
    terms = refs[:-2]
    mass = mass_of(terms[-2:], heights[-1])
    mass_ref[...] = mass
    inverse = 1.0 / mass
    start = 0
    for j, height in enumerate(heights):
        total = total_of(terms[2 * j : 2 * j + 2], height)
        out_ref[:, pl.ds(start, height)] = (total * inverse).T
        start += height


def body(embeddings, level_one, centroids):
    groups, peers = lax.axis_size("grp"), lax.axis_size("dev")
    routes = Routes(groups, peers)
    ring = routes.ring
    count, depth = embeddings.shape
    capacity = 2 * count // groups
    slots = groups * capacity
    owned = centroids.shape[0]
    clusters = owned * peers
    parts = 2

    small = max(16, owned * 6 // 256 * 16)
    swapped = send(centroids, routes.swap)

    place = call(
        rank_kernel,
        shape(-(-groups // 8) * 8, count, dtype=jnp.int32),
        [level_one.reshape(1, count)],
        name="rank_rows",
    )

    def pick(d, after=()):
        return call(
            functools.partial(pick_kernel, which=d),
            shape(capacity, depth),
            [place, embeddings],
            after=after,
            name="pick_rows",
        )

    direct = list(range(groups // 2, 0, -1))
    distant = list(range(groups // 2 + 1, groups))
    packed = {}
    for d in [*direct, *distant, 0]:
        packed[d] = pick(d, tuple(packed.values())[-1:])
    arrived = {d: send(packed[d], routes.cluster[d]) for d in direct}

    own = call(
        unit_kernel,
        (shape(small, depth), shape(owned - small, depth)),
        [swapped],
        after=[packed[0]],
        name="unit_centroids",
        cost_estimate=WAIT,
    )
    mine = [own]
    for s in range(1, ring):
        one, two = (send(p, routes.shift[1]) for p in mine[-1])
        if s < ring - 1:
            (one,) = tie([one], (), HALF)
            (two,) = tie([two], (one,), BRIEF)
        mine.append([one, two])
    for s in range(ring - 2):
        mine[s] = [tie([p], (q,), BRIEF)[0] for p, q in zip(mine[s], mine[s + 1])]
    mine[-2] = [tie([mine[-2][0]], mine[-1][:1], BRIEF)[0], mine[-2][1]]
    other = [[send(p, routes.core) for p in m] for m in mine[:-1]]

    waiting = tie([packed[d] for d in distant], [arrived[d] for d in direct], BRIEF)
    arrived |= {d: send(p, routes.cluster[d]) for d, p in zip(distant, waiting)}
    arrived[0] = packed[0]

    state_shapes = (
        shape(slots, depth),
        shape(1, slots, dtype=F32),
        shape(slots, clusters),
        shape(1, clusters, dtype=F32),
    )

    def absorb(state, raw, lines, columns):
        pieces = [p for s in columns for part in (mine, other) for p in part[s]]
        rows = [arrived[d] for d in raw]
        return call(
            functools.partial(
                weights_kernel,
                raw=raw,
                lines=lines,
                columns=columns,
                carried=bool(state),
                groups=groups,
            ),
            state_shapes,
            [*state, *rows, *pieces],
            alias={j: j for j in range(len(state))},
            name="weights",
        )

    near, early = [0, *sorted(direct)], list(range(ring - 1))
    state = absorb((), near, near, early[:-1])
    state = absorb(state, [], near, early[-1:])
    one, two = mine[-1]
    (one,) = tie([one], state[1:2], HALF)
    arrived.update(zip(distant, tie([arrived[d] for d in distant], (), BRIEF)))
    state = absorb(state, distant, distant, early)
    (two,) = tie([two], (one, state[1]), BRIEF)
    mine[-1] = [one, two]
    other.append([send(p, routes.core) for p in mine[-1]])
    rows, valid, weights, part = absorb(state, [], list(range(groups)), [ring - 1])
    turned = call(
        turn_kernel, shape(depth, slots), [arrived[d] for d in range(groups)], name="turn_rows"
    )

    def sweep(part, last):
        chip = call(
            join_kernel,
            shape(1, clusters, dtype=F32),
            [part, send(part, routes.core)],
            name="join_cores",
        )
        near = [send(chip, routes.both[t]) for t in range(1, ring // 2)]
        totals = [chip, send(chip, routes.shift[ring // 2])]
        for value in near:
            totals += [value, send(value, routes.core)]
        outs = (shape(1, clusters, dtype=F32),)
        if last:
            outs = (shape(1, slots, dtype=F32), *outs)
        return call(
            functools.partial(sweep_kernel, ring=ring, last=last),
            outs,
            [valid, weights, *totals],
            scratch_shapes=() if last else (pltpu.VMEM((1, clusters), F32),),
            name="last_sweep" if last else "sweep",
        )

    for _ in range(SWEEPS - 1):
        (part,) = sweep(part, last=False)
    row_scale, column_scale = sweep(part, last=True)

    heights = [depth * 4 // 8, depth - depth * 4 // 8]
    starts = [0, heights[0]]
    tall = [heights[0], heights[1] + 16]

    masses = []

    def numerator(s, j, after):
        fresh = scaled[j] is None
        args = [turned, weights, row_scale] if fresh else [scaled[j], weights]
        args = [*args, column_scale]
        if tall[j] > heights[j]:
            if not masses:
                masses.append(
                    call(
                        mass_kernel,
                        shape(1, clusters, dtype=F32),
                        [row_scale, column_scale, weights],
                        after=after,
                        name="masses",
                    )
                )
            args += masses
        outs = (shape(tall[j], owned),) * 2
        if fresh:
            outs = (shape(heights[j], slots), *outs)
        outs = call(
            functools.partial(
                numerator_kernel,
                chunk=s,
                first=starts[j],
                height=heights[j],
                fresh=fresh,
                extra=tall[j] - heights[j],
            ),
            outs,
            args,
            after=after,
            name="numerator",
            cost_estimate=cost(heights[j], 2 * owned, slots),
        )
        if fresh:
            scaled[j] = outs[0]
        return outs[-2], outs[-1]

    def combine(j, terms, after=()):
        return call(
            functools.partial(combine_kernel, height=heights[j]),
            shape(tall[j], owned),
            terms,
            after=after,
            name="combine",
            cost_estimate=BRIEF if j else TURN,
        )

    scaled = [None] * parts
    first, *others = [*range(1, ring), 0]
    pairs, moving, kept = {}, [()] * parts, [()] * parts

    def sums_of(s, after):
        for j in range(parts):
            kept_part, sent_part = numerator(s, j, after)
            pairs[s, j] = (kept_part, send(sent_part, routes.core))
            if s == first:
                after = (kept_part,)

    def step(s, after):
        route = routes.home if s == ring - 1 else routes.shift[1]
        sent = []
        for j in range(parts):
            added = combine(j, (*moving[j], *pairs[s, j]), after)
            moving[j] = (send(added, route),)
            sent.append(added)
            if s != first:
                after = (added,)
        return tuple(sent)

    after = ()
    for j in range(parts):
        kept_part, sent_part = numerator(first, j, after)
        pair = (kept_part, send(sent_part, routes.core))
        after += (combine(j, pair),)
        moving[j] = (send(after[-1], routes.home if ring == 2 else routes.shift[1]),)
    for s in others:
        sums_of(s, after)
    after = tuple(pairs[s, j][0] for s in others for j in range(parts))
    for s in others[:-1]:
        after = step(s, after)
        if s == others[0]:
            for j in range(parts):
                kept[j] = send(combine(j, pairs[0, j], after), routes.swap)

    (arrived_first,) = tie(moving[0], (), TURN)
    moving[0] = (arrived_first,)
    updated, mass = call(
        functools.partial(finish_kernel, heights=heights),
        (shape(owned, depth, dtype=F32), shape(1, owned, dtype=F32)),
        [t for j in range(parts) for t in (moving[j][0], kept[j])],
        name="finish",
    )
    return updated, mass.reshape(owned)


def solution(mesh):
    in_specs = (P(AXES, None), P(AXES, None), P(AXES, None))
    out_specs = (P(AXES, None), P(AXES))
    return jax.shard_map(body, mesh=mesh, in_specs=in_specs, out_specs=out_specs, check_vma=False)
```
